256 devices in a mesh: seq: 16 (over x, y_hi, core), dp: 16 (over z, y_lo).
Axes of the slice: x: 4, y: 4 (y_hi: 2, y_lo: 2; y = y_hi * 2 + y_lo), z: 8, core: 2. Of those that a mesh axis runs over, the one named last changes fastest.
Arguments:
- frames: bfloat16 [16, 2048, 1024], P('dp', 'seq'), may hold values from -6 to 6
- lengths: int32 [16], P('dp'), may hold values from 1024 to 2048, as said below
- stretch_sizes: int32 [16], P('dp'), may hold values from 8 to 32, as said below
- look_ahead: int32 [16], P('dp'), may hold values from 1 to 8, as said below
- norm_one: float32 [1024], replicated, may hold values from 0.5 to 1.5
- norm_two: float32 [1024], replicated, may hold values from 0.5 to 1.5
- w_query: bfloat16 [1024, 1024], replicated, may hold values from -8 to 8
- w_key: bfloat16 [1024, 1024], replicated, may hold values from -1 to 1
- w_value: bfloat16 [1024, 1024], replicated, may hold values from -0.1875 to 0.1875
- w_out: bfloat16 [1024, 1024], replicated, may hold values from -0.1875 to 0.1875
- conv_kernel: bfloat16 [31, 1024], replicated, may hold values from -1 to 1
Outputs:
- full_output: bfloat16 [16, 2048, 1024], P('dp', 'seq')
- stretch_output: bfloat16 [16, 2048, 1024], P('dp', 'seq')
- kernel_grad: float32 [31, 1024], replicated
The draws below stay inside these ranges and needn't reach their ends.
Inputs may be any that keep to these rules, and one draw needn't show every extreme that they name: `lengths`: utterance 0 has all 2048 frames. `stretch_sizes`: utterance 0 has stretch size 32. `look_ahead`: utterance 0 has preview 8.
All inputs are finite; a program needn't handle non-finite values.
Results may differ from the reference program's by a relative error of at most 0.0045.
The reference program's roundings to bfloat16 on the way (of `normed`, `weights`, `context` and `conv_input`) count: a program that leaves them out, or rounds other values in their place, can miss the bound.
Values may be sent and summed in bfloat16 or wider, within the bound.
No kernel may reach another device: no remote copies, remote signals or barrier semaphores. Data moves between devices by JAX's collectives and lax.ppermute only.
A program may use at most 128 MiB of HBM per device.

```python
import jax
import jax.numpy as jnp
from jax import lax

D = 1024
HEADS = 16
KERNEL = 31
LEFT = 64
HALO = 128
STRETCH_MAX = 32
LOOK_MAX = 8
FRAMES = 2048
UTTS = 16


def query_key_base(key):
    key_weight = jax.random.normal(jax.random.fold_in(key, 21), (D, D), jnp.float32) * D ** (-0.5)
    query_weight = jax.random.normal(jax.random.fold_in(key, 22), (D, D), jnp.float32) * D ** (-0.5)
    return (query_weight, key_weight)


def draw_w_key(key, part):
    query_weight, key_weight = query_key_base(key)
    return jnp.clip(key_weight, -1.0, 1.0).astype(jnp.bfloat16)


def draw_w_query(key, part):
    query_weight, key_weight = query_key_base(key)
    return jnp.clip(query_weight, -8.0, 8.0).astype(jnp.bfloat16)


def draw_frames(key, part):
    values = jax.random.normal(jax.random.fold_in(key, 32), (UTTS, FRAMES, D), jnp.float32)
    return jnp.clip(values, -6.0, 6.0).astype(jnp.bfloat16)


def draw_lengths(key, part):
    drawn = jax.random.randint(jax.random.fold_in(key, 41), (UTTS,), FRAMES // 2, FRAMES + 1)
    return drawn.at[0].set(FRAMES).astype(jnp.int32)


def draw_stretch_sizes(key, part):
    drawn = jax.random.randint(jax.random.fold_in(key, 42), (UTTS,), 8, STRETCH_MAX + 1)
    return drawn.at[0].set(STRETCH_MAX).astype(jnp.int32)


def draw_look_ahead(key, part):
    drawn = jax.random.randint(jax.random.fold_in(key, 43), (UTTS,), 1, LOOK_MAX + 1)
    return drawn.at[0].set(LOOK_MAX).astype(jnp.int32)


def bell_draw(stream_key, shape, width, reach, kind=jnp.bfloat16):
    return jnp.clip(width * jax.random.normal(stream_key, shape, jnp.float32), -reach, reach).astype(kind)


def setup_inputs(seed: int = 0) -> dict:
    streams_of = jax.random.split(jax.random.key(seed), 12)
    return {
        "frames": draw_frames(jax.random.fold_in(streams_of[11], 71), 0),
        "lengths": draw_lengths(jax.random.fold_in(streams_of[11], 71), 0),
        "stretch_sizes": draw_stretch_sizes(jax.random.fold_in(streams_of[11], 71), 0),
        "look_ahead": draw_look_ahead(jax.random.fold_in(streams_of[11], 71), 0),
        "norm_one": jnp.clip(1.0 + 0.1 * jax.random.normal(streams_of[4], (D,), jnp.float32), 0.5, 1.5),
        "norm_two": jnp.clip(1.0 + 0.1 * jax.random.normal(streams_of[5], (D,), jnp.float32), 0.5, 1.5),
        "w_query": draw_w_query(jax.random.fold_in(streams_of[11], 71), 0),
        "w_key": draw_w_key(jax.random.fold_in(streams_of[11], 71), 0),
        "w_value": bell_draw(streams_of[8], (D, D), D ** -0.5, 0.1875),
        "w_out": bell_draw(streams_of[9], (D, D), D ** -0.5, 0.1875),
        "conv_kernel": bell_draw(streams_of[10], (KERNEL, D), KERNEL ** -0.5, 1.0),
    }


EPSILON = 1e-05
FLOOR_SCORE = -1e+30

def layer_norm(values, gain_vector):
    values = values.astype(jnp.float32)
    center = values - lax.optimization_barrier(jnp.mean(values, axis=-1, keepdims=True))
    spread = lax.optimization_barrier(jnp.mean(center * center, axis=-1, keepdims=True))
    return center * lax.rsqrt(spread + EPSILON) * gain_vector.astype(jnp.float32)

def masked_attention(query3, key3, value3, visible, scale):
    scores = jnp.einsum('qhe,khe->hqk', query3.astype(jnp.float32), key3.astype(jnp.float32)) * scale
    scores = jnp.where(visible[None], scores, FLOOR_SCORE)
    highest = lax.optimization_barrier(jnp.max(scores, axis=-1, keepdims=True))
    expo = jnp.where(visible[None], jnp.exp(scores - highest), 0.0)
    totals = lax.optimization_barrier(jnp.sum(expo, axis=-1))
    weights = expo.astype(jnp.bfloat16)
    mixed = jnp.einsum('hqk,khe->qhe', weights.astype(jnp.float32), value3.astype(jnp.float32))
    return (mixed / totals.T[:, :, None]).reshape(query3.shape[0], -1).astype(jnp.bfloat16)

def reference(frames, lengths, stretch_sizes, look_ahead, norm_one, norm_two, w_query, w_key, w_value, w_out, conv_kernel):
    depth = D // HEADS
    scale = float(depth) ** (-0.5)
    block_rows = 512
    block_count = FRAMES // block_rows
    kernel_taps = conv_kernel.astype(jnp.float32)

    def utterance(items):
        source, length, stretch, lookup = items
        normed = layer_norm(source, norm_one).astype(jnp.bfloat16)
        query = jnp.dot(normed, w_query, preferred_element_type=jnp.float32).astype(jnp.bfloat16).reshape(FRAMES, HEADS, depth)
        keys = jnp.dot(normed, w_key, preferred_element_type=jnp.float32).astype(jnp.bfloat16).reshape(FRAMES, HEADS, depth)
        values = jnp.dot(normed, w_value, preferred_element_type=jnp.float32).astype(jnp.bfloat16).reshape(FRAMES, HEADS, depth)
        every_pos = jnp.arange(FRAMES, dtype=jnp.int32)

        def full_block(index):
            start = index * block_rows
            query_block = lax.dynamic_slice_in_dim(query, start, block_rows, 0)
            query_pos = start + jnp.arange(block_rows, dtype=jnp.int32)
            visible = (every_pos[None, :] < length) | (every_pos[None, :] == query_pos[:, None])
            return masked_attention(query_block, keys, values, visible, scale)
        keys_pad = jnp.pad(keys, ((HALO, HALO), (0, 0), (0, 0)))
        values_pad = jnp.pad(values, ((HALO, HALO), (0, 0), (0, 0)))

        def stretch_block(index):
            start = index * block_rows
            span = block_rows + 2 * HALO
            query_block = lax.dynamic_slice_in_dim(query, start, block_rows, 0)
            key_block = lax.dynamic_slice_in_dim(keys_pad, start, span, 0)
            value_block = lax.dynamic_slice_in_dim(values_pad, start, span, 0)
            query_pos = start + jnp.arange(block_rows, dtype=jnp.int32)
            key_pos = start - HALO + jnp.arange(span, dtype=jnp.int32)
            begin = query_pos // stretch * stretch
            inside = (key_pos[None, :] >= begin[:, None] - LEFT) & (key_pos[None, :] < begin[:, None] + stretch + lookup)
            inside = inside & (key_pos[None, :] >= 0) & (key_pos[None, :] < length)
            visible = inside | (key_pos[None, :] == query_pos[:, None])
            return masked_attention(query_block, key_block, value_block, visible, scale)
        blocks = jnp.arange(block_count, dtype=jnp.int32)
        context_full = lax.map(full_block, blocks).reshape(FRAMES, D)
        context_stretch = lax.map(stretch_block, blocks).reshape(FRAMES, D)
        valid = (every_pos < length).astype(jnp.float32)

        def finish(context, causal):
            residual = source.astype(jnp.float32) + jnp.dot(context, w_out, preferred_element_type=jnp.float32)
            conv_input = (layer_norm(residual, norm_two) * valid[:, None]).astype(jnp.bfloat16)
            if causal:
                padded = jnp.pad(conv_input, ((KERNEL - 1, 0), (0, 0)))
            else:
                padded = jnp.pad(conv_input, ((KERNEL // 2, KERNEL // 2), (0, 0)))
            conv = jnp.zeros((FRAMES, D), jnp.float32)
            for offset in range(KERNEL):
                conv = conv + kernel_taps[offset] * padded[offset:offset + FRAMES].astype(jnp.float32)
            return (residual + jax.nn.silu(conv), conv, padded)
        output_full, _, _ = finish(context_full, False)
        output_stretch, conv_stretch, padded_stretch = finish(context_stretch, True)
        push = 2.0 * (output_stretch - output_full) * valid[:, None] / jnp.sqrt(length.astype(jnp.float32))
        sigma = jax.nn.sigmoid(conv_stretch)
        slope = push * sigma * (1.0 + conv_stretch * (1.0 - sigma))
        grads = jnp.stack([lax.optimization_barrier(jnp.sum(slope * padded_stretch[offset:offset + FRAMES].astype(jnp.float32), axis=0)) for offset in range(KERNEL)])
        return (output_full.astype(jnp.bfloat16), output_stretch.astype(jnp.bfloat16), grads)
    full_output, stretch_output, grads = lax.map(utterance, (frames, lengths, stretch_sizes, look_ahead))
    return (full_output, stretch_output, lax.optimization_barrier(jnp.sum(grads, axis=0)))
```

```python
import functools

import jax
import jax.numpy as jnp
from jax import lax
from jax.experimental import pallas as pl
from jax.experimental.pallas import tpu as pltpu
from jax.sharding import PartitionSpec as P

HEADS = 16
DEPTH = 64
KERNEL = 31
LEFT = 64
EPSILON = 1e-05
FLOOR_SCORE = -1e30
BEFORE = 32
AFTER = 16
LANES = 128
F32 = jnp.float32
BF16 = jnp.bfloat16


def norm_rows(values, gain):
    center = values - jnp.mean(values, axis=-1, keepdims=True)
    spread = jnp.mean(center * center, axis=-1, keepdims=True)
    return center * lax.rsqrt(spread + EPSILON) * gain


def low_lanes(rows):
    return lax.broadcasted_iota(jnp.int32, (rows, LANES), 1) < DEPTH


def half_turn(value):
    return pltpu.roll(value, DEPTH, 1)


def dot_rows(left, right):
    return lax.dot_general(left, right, (((1,), (1,)), ((), ())), preferred_element_type=F32)


def project_kernel(frames_ref, gain_ref, wq_ref, wk_ref, wv_ref, out_ref, normed_ref):
    rows = frames_ref.shape[0]
    half = rows // 2

    @pl.when(pl.program_id(0) == 0)
    def _():
        normed_ref[...] = norm_rows(frames_ref[...].astype(F32), gain_ref[...]).astype(BF16)

    normed = normed_ref[...]
    query = jnp.dot(normed, wq_ref[...], preferred_element_type=F32) * (DEPTH**-0.5)
    key = jnp.dot(normed, wk_ref[...], preferred_element_type=F32)
    value = jnp.dot(normed, wv_ref[...], preferred_element_type=F32)
    low = low_lanes(rows)
    low_half = low_lanes(half)
    for pair in range(out_ref.shape[0] // 2):
        cols = slice(pair * LANES, (pair + 1) * LANES)
        k, v, q = key[:, cols], value[:, cols], query[:, cols]
        kr, vr, qr = half_turn(k), half_turn(v), half_turn(q)
        out_ref[2 * pair, :rows] = jnp.where(low, k, vr).astype(BF16)
        out_ref[2 * pair + 1, :rows] = jnp.where(low, kr, v).astype(BF16)
        out_ref[2 * pair, rows:] = jnp.where(low_half, q[:half], qr[half:]).astype(BF16)
        out_ref[2 * pair + 1, rows:] = jnp.where(low_half, qr[:half], q[half:]).astype(BF16)


def project(frames, gain, wq, wk, wv):
    rows, width = frames.shape
    steps = 4
    cols = width // steps
    heads = HEADS // steps
    weight = pl.BlockSpec((width, cols), lambda i: (0, i))
    return pl.pallas_call(
        project_kernel,
        grid=(steps,),
        in_specs=[
            pl.BlockSpec((rows, width), lambda i: (0, 0)),
            pl.BlockSpec((1, width), lambda i: (0, 0)),
            weight,
            weight,
            weight,
        ],
        out_specs=pl.BlockSpec((heads, rows + rows // 2, LANES), lambda i: (i, 0, 0)),
        out_shape=jax.ShapeDtypeStruct((HEADS, rows + rows // 2, LANES), BF16),
        scratch_shapes=[pltpu.VMEM((rows, width), BF16)],
        compiler_params=pltpu.CompilerParams(vmem_limit_bytes=32 << 20),
        name="project",
    )(frames, gain, wq, wk, wv)


def attend_kernel(
    length_ref, stretch_ref, look_ref, packed_ref, out_ref, kv_ref, q_ref, bias_ref, s0_ref, s1_ref, ctx_ref
):
    blocks, packed_rows, _ = packed_ref.shape
    rows = packed_rows * 2 // 3
    half = rows // 2
    total = blocks * rows
    length = length_ref[0]
    stretch = stretch_ref[0].astype(F32)
    look = look_ref[0].astype(F32)
    length_f = length.astype(F32)
    low_half = low_lanes(half)
    kv_ref[:rows] = jnp.zeros((rows, LANES), BF16)
    kv_ref[rows + total :] = jnp.zeros((rows, LANES), BF16)
    for block in range(blocks):
        kv_ref[(block + 1) * rows : (block + 2) * rows] = packed_ref[block, :rows]
        q = packed_ref[block, rows:].astype(F32)
        q_ref[block * rows : block * rows + half] = jnp.where(low_half, q, 0.0).astype(BF16)
        q_ref[block * rows + half : (block + 1) * rows] = jnp.where(low_half, half_turn(q), 0.0).astype(BF16)
    key_pos = lax.broadcasted_iota(jnp.int32, (8, total), 1)
    bias_ref[...] = jnp.where(key_pos < length, 0.0, FLOOR_SCORE)
    ctx_ref[:BEFORE] = jnp.zeros((BEFORE, LANES), BF16)
    ctx_ref[BEFORE + total :] = jnp.zeros((AFTER, LANES), BF16)

    def at(index):
        return pl.ds(pl.multiple_of(index * rows, rows), rows)

    def score(index, s_ref):
        s_ref[...] = dot_rows(q_ref[at(index)], kv_ref[rows : rows + total]) + bias_ref[0:1]

    def finish(index, s_ref):
        start = pl.multiple_of(index * rows, rows)
        near = kv_ref[pl.ds(start, 3 * rows)]
        raw = dot_rows(q_ref[at(index)], near)
        row = lax.broadcasted_iota(jnp.int32, (rows, LANES), 0)
        lane = lax.broadcasted_iota(jnp.int32, (rows, LANES), 1)
        seen = (lane == row) | (lane + start < length)
        s_ref[:, at(index)] = jnp.where(seen, raw[:, rows : 2 * rows], FLOOR_SCORE)
        s = s_ref[...]
        highest = jnp.max(s, axis=-1, keepdims=True)
        expo = jnp.exp(s - highest)
        totals = jnp.sum(expo, axis=-1, keepdims=True)
        mixed = jnp.dot(expo.astype(BF16), kv_ref[rows : rows + total], preferred_element_type=F32)
        full = mixed / totals

        pos = (row + start).astype(F32)
        begin = jnp.floor((pos + 0.5) / stretch) * stretch
        first = jnp.maximum(begin - LEFT, 0.0)
        last = jnp.minimum(begin + stretch + look, length_f)
        parts = []
        for part in range(3):
            key_at = (lane + start + (part - 1) * rows).astype(F32)
            inside = (key_at >= first) & (key_at < last)
            if part == 1:
                inside = inside | (lane == row)
            parts.append(jnp.where(inside, raw[:, part * rows : (part + 1) * rows], FLOOR_SCORE))
        s = jnp.concatenate(parts, axis=1)
        highest = jnp.max(s, axis=-1, keepdims=True)
        expo = jnp.exp(s - highest)
        totals = jnp.sum(expo, axis=-1, keepdims=True)
        mixed = jnp.dot(expo.astype(BF16), near, preferred_element_type=F32)
        near_context = mixed / totals
        both = jnp.where(lane < DEPTH, half_turn(full), near_context)
        ctx_ref[pl.ds(pl.multiple_of(start + BEFORE, BEFORE), rows)] = both.astype(BF16)

    score(0, s0_ref)

    def body(step, carry):
        score(2 * step + 1, s1_ref)
        finish(2 * step, s0_ref)
        score(jnp.minimum(2 * step + 2, blocks - 1), s0_ref)
        finish(2 * step + 1, s1_ref)
        return carry

    lax.fori_loop(0, blocks // 2, body, 0)
    for block in range(blocks):
        out_ref[block] = ctx_ref[block * rows : block * rows + BEFORE + rows + AFTER]


def attend(length, stretch, look, packed):
    blocks, packed_rows, _ = packed.shape
    rows = packed_rows * 2 // 3
    total = blocks * rows
    smem = pl.BlockSpec(memory_space=pltpu.SMEM)
    vmem = pl.BlockSpec(memory_space=pltpu.VMEM)
    return pl.pallas_call(
        attend_kernel,
        in_specs=[smem, smem, smem, vmem],
        out_specs=vmem,
        out_shape=jax.ShapeDtypeStruct((blocks, BEFORE + rows + AFTER, LANES), BF16),
        scratch_shapes=[
            pltpu.VMEM((total + 2 * rows, LANES), BF16),
            pltpu.VMEM((total, LANES), BF16),
            pltpu.VMEM((8, total), F32),
            pltpu.VMEM((rows, total), F32),
            pltpu.VMEM((rows, total), F32),
            pltpu.VMEM((BEFORE + total + AFTER, LANES), BF16),
        ],
        compiler_params=pltpu.CompilerParams(vmem_limit_bytes=32 << 20),
        name="attend",
    )(length, stretch, look, packed)


def finish_kernel(
    place_ref,
    length_ref,
    ctx_ref,
    before_ref,
    frames_ref,
    after_ref,
    wo_ref,
    gain_ref,
    taps_ref,
    full_ref,
    near_ref,
    grad_ref,
    c_ref,
    res_ref,
    x_ref,
):
    rows, width = frames_ref.shape
    ext = BEFORE + rows + AFTER
    low = low_lanes(ext)
    for pair in range(HEADS // 2):
        cols = slice(pair * LANES, (pair + 1) * LANES)
        one, two = ctx_ref[2 * pair].astype(F32), ctx_ref[2 * pair + 1].astype(F32)
        c_ref[:ext, cols] = jnp.where(low, one, half_turn(two)).astype(BF16)
        c_ref[ext:, cols] = jnp.where(low, half_turn(one), two).astype(BF16)
    length = length_ref[0]
    source = jnp.concatenate([before_ref[...], frames_ref[...], after_ref[...]], axis=0).astype(F32)
    res_ref[...] = jnp.dot(c_ref[...], wo_ref[...], preferred_element_type=F32)
    pos = lax.broadcasted_iota(jnp.int32, (ext, 1), 0) + (place_ref[0] * rows - BEFORE)
    valid = (pos >= 0) & (pos < length)
    for part in range(2):
        span = slice(part * ext, (part + 1) * ext)
        residual = source + res_ref[span]
        res_ref[span] = residual
        normed = norm_rows(residual, gain_ref[...])
        x_ref[span] = jnp.where(valid, normed, 0.0).astype(BF16).astype(F32)
    inner = lax.broadcasted_iota(jnp.int32, (rows, 1), 0) + place_ref[0] * rows
    factor = jnp.where(inner < length, 2.0 / jnp.sqrt(jnp.full((rows, 1), length.astype(F32))), 0.0)

    def convolve(first, cols):
        total = jnp.zeros((rows, LANES), F32)
        for turn in range(8):
            offsets = [k for k in range(KERNEL) if (first + k) % 8 == turn]
            low_at = first + offsets[0]
            count = offsets[-1] - offsets[0] + rows
            piece = x_ref[low_at : low_at + count, cols]
            for k in offsets:
                skip = k - offsets[0]
                total = total + taps_ref[k : k + 1, cols] * piece[skip : skip + rows]
        return total

    def column(step, carry):
        cols = pl.ds(pl.multiple_of(step * LANES, LANES), LANES)
        conv_full = convolve(BEFORE - KERNEL // 2, cols)
        sig_full = 1.0 / (1.0 + jnp.exp(-conv_full))
        out_full = res_ref[BEFORE : BEFORE + rows, cols] + conv_full * sig_full
        full_ref[:, cols] = out_full.astype(BF16)
        near_first = ext + BEFORE - (KERNEL - 1)
        conv_near = convolve(near_first, cols)
        sig_near = 1.0 / (1.0 + jnp.exp(-conv_near))
        out_near = res_ref[ext + BEFORE : ext + BEFORE + rows, cols] + conv_near * sig_near
        near_ref[:, cols] = out_near.astype(BF16)
        slope = (out_near - out_full) * factor * (sig_near * (1.0 + conv_near * (1.0 - sig_near)))
        for turn in range(8):
            offsets = [k for k in range(KERNEL) if (near_first + k) % 8 == turn]
            low_at = near_first + offsets[0]
            count = offsets[-1] - offsets[0] + rows
            piece = x_ref[low_at : low_at + count, cols]
            for k in offsets:
                skip = k - offsets[0]
                term = jnp.sum(slope * piece[skip : skip + rows], axis=0, keepdims=True)
                grad_ref[2 * step + k // 16, k % 16 : k % 16 + 1] = term
        grad_ref[2 * step + 1, 15:16] = jnp.zeros((1, LANES), F32)
        return carry

    lax.fori_loop(0, width // LANES, column, 0)


def finish(place, length, ctx, before, frames, after, wo, gain, taps):
    rows, width = frames.shape
    ext = BEFORE + rows + AFTER
    smem = pl.BlockSpec(memory_space=pltpu.SMEM)
    vmem = pl.BlockSpec(memory_space=pltpu.VMEM)
    return pl.pallas_call(
        finish_kernel,
        in_specs=[smem, smem] + [vmem] * 7,
        out_specs=[vmem] * 3,
        out_shape=[
            jax.ShapeDtypeStruct((rows, width), BF16),
            jax.ShapeDtypeStruct((rows, width), BF16),
            jax.ShapeDtypeStruct((width // 64, 16, LANES), F32),
        ],
        scratch_shapes=[
            pltpu.VMEM((2 * ext, width), BF16),
            pltpu.VMEM((2 * ext, width), F32),
            pltpu.VMEM((2 * ext, width), F32),
        ],
        compiler_params=pltpu.CompilerParams(vmem_limit_bytes=40 << 20),
        name="finish",
    )(place, length, ctx, before, frames, after, wo, gain, taps)


def swap(value, axis):
    return lax.all_to_all(value, axis, 0, 0, tiled=True)


def spread_out(value, axis):
    size = lax.axis_size(axis)
    return swap(jnp.broadcast_to(value[None], (size,) + value.shape), axis)


def per_device(
    frames,
    lengths,
    stretch_sizes,
    look_ahead,
    norm_one,
    norm_two,
    w_query,
    w_key,
    w_value,
    w_out,
    conv_kernel,
):
    source = frames[0]
    rows, width = source.shape
    size = lax.axis_size("seq")
    place = lax.axis_index("seq").reshape(1).astype(jnp.int32)
    up = [(i, i + 1) for i in range(size - 1)]
    down = [(j, i) for i, j in up]
    before = lax.ppermute(source[rows - BEFORE :], "seq", up)
    after = lax.ppermute(source[:AFTER], "seq", down)
    taps = jnp.pad(conv_kernel.astype(F32), ((0, 1), (0, 0)))
    packed = project(source, norm_one[None], w_query, w_key, w_value)
    packed = swap(packed, "seq")
    ctx = attend(lengths, stretch_sizes, look_ahead, packed)
    ctx = swap(ctx, "seq")
    full, near, grad = finish(
        place, lengths, ctx, before, source, after, w_out, norm_two[None], taps
    )
    piece = jnp.sum(swap(grad, "seq"), axis=0)
    piece = jnp.sum(spread_out(piece, "dp"), axis=0)
    grads = spread_out(piece, "seq")
    grads = grads.reshape(width // LANES, 32, LANES).transpose(1, 0, 2).reshape(32, width)
    return full[None], near[None], grads[:KERNEL]


def solution(mesh):
    in_specs = (P("dp", "seq", None), P("dp"), P("dp"), P("dp"), P(), P(), P(), P(), P(), P(), P())
    out_specs = (P("dp", "seq", None), P("dp", "seq", None), P())
    return jax.shard_map(
        per_device, mesh=mesh, in_specs=in_specs, out_specs=out_specs, check_vma=False
    )
```

```python
import jax
import jax.numpy as jnp
from jax import lax
from jax.experimental import pallas as pl
from jax.experimental.pallas import tpu as pltpu
from jax.sharding import PartitionSpec as P

HEADS = 16
DEPTH = 64
KERNEL = 31
LEFT = 64
EPSILON = 1e-05
FLOOR_SCORE = -1e30
BEFORE = 32
AFTER = 16
LANES = 128
PIECES = 4
QUERIES = 256
SHORTEST = 1024
F32 = jnp.float32
BF16 = jnp.bfloat16
SMEM_SPEC = pl.BlockSpec(memory_space=pltpu.SMEM)
VMEM_SPEC = pl.BlockSpec(memory_space=pltpu.VMEM)


def cost(flops, accessed):
    return pl.CostEstimate(flops=flops, bytes_accessed=accessed, transcendentals=0)


def norm_rows(values, gain):
    center = values - jnp.mean(values, axis=-1, keepdims=True)
    spread = jnp.mean(center * center, axis=-1, keepdims=True)
    return center * lax.rsqrt(spread + EPSILON) * gain


def low_lanes(rows):
    return lax.broadcasted_iota(jnp.int32, (rows, LANES), 1) < DEPTH


def half_turn(value):
    return pltpu.roll(value, DEPTH, 1)


def dot_rows(left, right):
    return lax.dot_general(left, right, (((1,), (1,)), ((), ())), preferred_element_type=F32)


def project_kernel(frames_hbm, gain_ref, wq_hbm, wk_hbm, wv_hbm, out_ref, frames_ref, w_ref, sem):
    rows, width = frames_ref.shape
    half = rows // 2
    deep = width // PIECES
    first = pltpu.make_async_copy(frames_hbm, frames_ref, sem.at[3 * PIECES])
    first.start()
    copies = []
    for index, hbm in enumerate((wk_hbm, wv_hbm, wq_hbm)):
        for piece in range(PIECES):
            span = slice(piece * deep, (piece + 1) * deep)
            copy = pltpu.make_async_copy(
                hbm.at[span], w_ref.at[index, span], sem.at[index * PIECES + piece]
            )
            copy.start()
            copies.append(copy)
    first.wait()
    normed = norm_rows(frames_ref[...].astype(F32), gain_ref[...]).astype(BF16)
    products = []
    for index in range(3):
        total = None
        for piece in range(PIECES):
            span = slice(piece * deep, (piece + 1) * deep)
            copies[index * PIECES + piece].wait()
            term = jnp.dot(normed[:, span], w_ref[index, span], preferred_element_type=F32)
            total = term if total is None else total + term
        products.append(total)
    key, value, query = products
    query = query * (DEPTH**-0.5)
    low = low_lanes(rows)
    low_half = low_lanes(half)
    for pair in range(HEADS // 2):
        cols = slice(pair * LANES, (pair + 1) * LANES)
        k, v, q = key[:, cols], value[:, cols], query[:, cols]
        kr, vr, qr = half_turn(k), half_turn(v), half_turn(q)
        out_ref[2 * pair, :rows] = jnp.where(low, k, vr).astype(BF16)
        out_ref[2 * pair + 1, :rows] = jnp.where(low, kr, v).astype(BF16)
        out_ref[2 * pair, rows:] = jnp.where(low_half, q[:half], qr[half:]).astype(BF16)
        out_ref[2 * pair + 1, rows:] = jnp.where(low_half, qr[:half], q[half:]).astype(BF16)


def project(frames, gain, wq, wk, wv):
    rows, width = frames.shape
    hbm = pl.BlockSpec(memory_space=pltpu.HBM)
    return pl.pallas_call(
        project_kernel,
        in_specs=[hbm, VMEM_SPEC, hbm, hbm, hbm],
        out_specs=VMEM_SPEC,
        out_shape=jax.ShapeDtypeStruct((HEADS, rows + rows // 2, LANES), BF16),
        scratch_shapes=[
            pltpu.VMEM((rows, width), BF16),
            pltpu.VMEM((3, width, width), BF16),
            pltpu.SemaphoreType.DMA((3 * PIECES + 1,)),
        ],
        compiler_params=pltpu.CompilerParams(vmem_limit_bytes=62 << 20),
        cost_estimate=cost(6 * rows * width * width, 6 * width * width),
        name="project",
    )(frames, gain, wq, wk, wv)


def row_softmax(scores):
    highest = jnp.max(scores, axis=-1, keepdims=True)
    expo = jnp.exp(scores - highest)
    return expo.astype(BF16), jnp.sum(expo, axis=-1, keepdims=True)


def attend_kernel(
    length_ref, stretch_ref, look_ref, packed_ref, out_ref,
    q_ref, bias_ref, s0_ref, s1_ref, full_ref, near_ref,
):
    blocks, packed_rows, _ = packed_ref.shape
    rows = packed_rows * 2 // 3
    half = rows // 2
    total = blocks * rows
    steps = total // QUERIES
    share = QUERIES // rows
    length = length_ref[0]
    length_f = length.astype(F32)
    stretch = stretch_ref[0].astype(F32)
    look = look_ref[0].astype(F32)
    low_half = low_lanes(half)
    for block in range(blocks):
        q = packed_ref[block, rows:].astype(F32)
        start = block * rows
        q_ref[start : start + half] = jnp.where(low_half, q, 0.0).astype(BF16)
        q_ref[start + half : start + rows] = jnp.where(low_half, half_turn(q), 0.0).astype(BF16)
    near_ref[:BEFORE] = jnp.zeros((BEFORE, LANES), BF16)
    full_ref[:AFTER] = jnp.zeros((AFTER, LANES), BF16)
    full_ref[AFTER + total :] = jnp.zeros((AFTER, LANES), BF16)
    key_pos = lax.broadcasted_iota(jnp.int32, (8, total), 1)
    bias_ref[...] = jnp.where(key_pos < length, 0.0, FLOOR_SCORE)
    row = lax.broadcasted_iota(jnp.int32, (rows, LANES), 0)
    lane = lax.broadcasted_iota(jnp.int32, (rows, LANES), 1)
    lane_f = lane.astype(F32)
    row_f = lax.broadcasted_iota(jnp.int32, (rows, 1), 0).astype(F32)

    def at(index):
        return pl.ds(pl.multiple_of(index * QUERIES, QUERIES), QUERIES)

    def keys(first, count):
        return jnp.concatenate([packed_ref[b, :rows] for b in range(first, first + count)], axis=0)

    def score(index, s_ref):
        q = q_ref[at(index)]
        always = SHORTEST // rows
        s_ref[:, :SHORTEST] = dot_rows(q, keys(0, always))
        s_ref[:, SHORTEST:] = dot_rows(q, keys(always, blocks - always)) + bias_ref[0:1, SHORTEST:]

    def own(index, s_ref):
        @pl.when((index + 1) * QUERIES > length)
        def _():
            for part in range(share):
                block = index * share + part
                start = pl.multiple_of(block * rows, rows)
                raw = dot_rows(q_ref[pl.ds(start, rows)], packed_ref[block, :rows])
                seen = (lane == row) | (lane + start < length)
                s_ref[part * rows : (part + 1) * rows, pl.ds(start, rows)] = jnp.where(
                    seen, raw, FLOOR_SCORE
                )

    def mix(index, s_ref):
        weights, totals = row_softmax(s_ref[...])
        mixed = jnp.dot(weights, keys(0, blocks), preferred_element_type=F32)
        full_ref[pl.ds(pl.multiple_of(index * QUERIES + AFTER, AFTER), QUERIES)] = half_turn(
            mixed / totals
        ).astype(BF16)

    def near(block):
        start = pl.multiple_of(block * rows, rows)
        base = (block * rows).astype(F32) if not isinstance(block, int) else float(block * rows)
        pos = row_f + base
        begin = jnp.floor((pos + 0.5) / stretch) * stretch
        first = jnp.broadcast_to(jnp.maximum(begin - LEFT, 0.0) - base, (rows, LANES))
        last = jnp.broadcast_to(jnp.minimum(begin + stretch + look, length_f) - base, (rows, LANES))
        around = (jnp.maximum(block - 1, 0), block, jnp.minimum(block + 1, blocks - 1))
        window = jnp.concatenate([packed_ref[b, :rows] for b in around], axis=0)
        raw = dot_rows(q_ref[pl.ds(start, rows)], window)
        parts = []
        for part in range(3):
            key_at = lane_f + float((part - 1) * rows)
            inside = (key_at >= first) & (key_at < last)
            if part == 1:
                inside = inside | (lane == row)
            parts.append(jnp.where(inside, raw[:, part * rows : (part + 1) * rows], FLOOR_SCORE))
        weights, totals = row_softmax(jnp.concatenate(parts, axis=1))
        mixed = jnp.dot(weights, window, preferred_element_type=F32)
        near_ref[pl.ds(pl.multiple_of(start + BEFORE, BEFORE), rows)] = (mixed / totals).astype(
            BF16
        )

    def nears(index):
        for part in range(share):
            near(index * share + part)

    score(0, s0_ref)
    own(0, s0_ref)

    def body(step, carry):
        score(2 * step + 1, s1_ref)
        mix(2 * step, s0_ref)
        nears(2 * step)
        own(2 * step + 1, s1_ref)
        score(2 * step + 2, s0_ref)
        mix(2 * step + 1, s1_ref)
        nears(2 * step + 1)
        own(2 * step + 2, s0_ref)
        return carry

    lax.fori_loop(0, steps // 2 - 1, body, 0)
    score(steps - 1, s1_ref)
    mix(steps - 2, s0_ref)
    nears(jnp.int32(steps - 2))
    own(steps - 1, s1_ref)
    mix(steps - 1, s1_ref)
    nears(jnp.int32(steps - 1))
    ext = BEFORE + rows
    low = low_lanes(ext)
    for block in range(blocks):
        span = slice(block * rows, block * rows + ext)
        out_ref[block] = jnp.where(
            low, full_ref[span].astype(F32), near_ref[span].astype(F32)
        ).astype(BF16)


def attend(length, stretch, look, packed):
    blocks, packed_rows, _ = packed.shape
    rows = packed_rows * 2 // 3
    total = blocks * rows
    return pl.pallas_call(
        attend_kernel,
        in_specs=[SMEM_SPEC] * 3 + [VMEM_SPEC],
        out_specs=VMEM_SPEC,
        out_shape=jax.ShapeDtypeStruct((blocks, BEFORE + rows, LANES), BF16),
        scratch_shapes=[
            pltpu.VMEM((total, LANES), BF16),
            pltpu.VMEM((8, total), F32),
            pltpu.VMEM((QUERIES, total), F32),
            pltpu.VMEM((QUERIES, total), F32),
            pltpu.VMEM((total + 2 * AFTER, LANES), BF16),
            pltpu.VMEM((BEFORE + total, LANES), BF16),
        ],
        compiler_params=pltpu.CompilerParams(vmem_limit_bytes=32 << 20),
        cost_estimate=cost(4 * total * (total + 3 * rows) * LANES, 2 << 20),
        name="attend",
    )(length, stretch, look, packed)


def turns(first):
    for turn in range(8):
        offsets = [k for k in range(KERNEL) if (first + k) % 8 == turn]
        yield offsets, first + offsets[0], offsets[-1] - offsets[0]


def convolve(x_ref, taps_ref, first, rows, cols):
    total = jnp.zeros((rows, LANES), F32)
    for offsets, low_at, extra in turns(first):
        piece = x_ref[low_at : low_at + extra + rows, cols]
        for k in offsets:
            skip = k - offsets[0]
            total = total + taps_ref[k : k + 1, cols] * piece[skip : skip + rows]
    return total


def finish_kernel(
    place_ref, length_ref, ctx_ref, before_ref, frames_ref, after_ref, wo_ref, gain_ref, taps_ref,
    full_ref, near_ref, grad_ref, c_ref, res_ref, x_ref,
):
    rows, width = frames_ref.shape
    ext = BEFORE + rows
    length = length_ref[0]
    start = place_ref[0] * rows
    low = low_lanes(ext)
    for pair in range(HEADS // 2):
        cols = slice(pair * LANES, (pair + 1) * LANES)
        one, two = ctx_ref[2 * pair].astype(F32), ctx_ref[2 * pair + 1].astype(F32)
        c_ref[:ext, cols] = jnp.where(low, one, half_turn(two)).astype(BF16)
        c_ref[ext:, cols] = jnp.where(low, half_turn(one), two).astype(BF16)
    frames = frames_ref[...]
    source = jnp.concatenate(
        [before_ref[BEFORE - AFTER :], frames, after_ref[...], before_ref[...], frames], axis=0
    ).astype(F32)
    residual = source + jnp.dot(c_ref[...], wo_ref[...], preferred_element_type=F32)
    res_ref[...] = residual
    normed = norm_rows(residual, gain_ref[...])
    line = lax.broadcasted_iota(jnp.int32, (2 * ext, 1), 0)
    pos = start + jnp.where(line < ext, line - AFTER, line - ext - BEFORE)
    valid = (pos >= 0) & (pos < length)
    x_ref[...] = jnp.where(valid, normed, 0.0).astype(BF16).astype(F32)
    inner = lax.broadcasted_iota(jnp.int32, (rows, 1), 0) + start
    factor = jnp.where(inner < length, 2.0 / jnp.sqrt(jnp.full((rows, 1), length.astype(F32))), 0.0)
    near_first = ext + BEFORE - (KERNEL - 1)

    def column(step, carry):
        cols = pl.ds(pl.multiple_of(step * LANES, LANES), LANES)
        conv = convolve(x_ref, taps_ref, AFTER - KERNEL // 2, rows, cols)
        out_full = res_ref[AFTER : AFTER + rows, cols] + conv / (1.0 + jnp.exp(-conv))
        full_ref[:, cols] = out_full.astype(BF16)
        conv = convolve(x_ref, taps_ref, near_first, rows, cols)
        sigma = 1.0 / (1.0 + jnp.exp(-conv))
        out_near = res_ref[ext + BEFORE :, cols] + conv * sigma
        near_ref[:, cols] = out_near.astype(BF16)
        slope = (out_near - out_full) * factor * (sigma * (1.0 + conv * (1.0 - sigma)))
        for offsets, low_at, extra in turns(near_first):
            piece = x_ref[low_at : low_at + extra + rows, cols]
            for k in offsets:
                skip = k - offsets[0]
                term = jnp.sum(slope * piece[skip : skip + rows], axis=0, keepdims=True)
                grad_ref[2 * step + k // 16, k % 16 : k % 16 + 1] = term
        grad_ref[2 * step + 1, 15:16] = jnp.zeros((1, LANES), F32)
        return carry

    lax.fori_loop(0, width // LANES, column, 0)


def finish(place, length, ctx, before, frames, after, wo, gain, taps):
    rows, width = frames.shape
    ext = BEFORE + rows
    return pl.pallas_call(
        finish_kernel,
        in_specs=[SMEM_SPEC] * 2 + [VMEM_SPEC] * 7,
        out_specs=[VMEM_SPEC] * 3,
        out_shape=[
            jax.ShapeDtypeStruct((rows, width), BF16),
            jax.ShapeDtypeStruct((rows, width), BF16),
            jax.ShapeDtypeStruct((width // 64, 16, LANES), F32),
        ],
        scratch_shapes=[
            pltpu.VMEM((2 * ext, width), BF16),
            pltpu.VMEM((2 * ext, width), F32),
            pltpu.VMEM((2 * ext, width), F32),
        ],
        compiler_params=pltpu.CompilerParams(vmem_limit_bytes=40 << 20),
        cost_estimate=cost(4 * ext * width * width, 6 << 20),
        name="finish",
    )(place, length, ctx, before, frames, after, wo, gain, taps)


def swap(value, axis):
    return lax.all_to_all(value, axis, 0, 0, tiled=True)


def spread_out(value, axis):
    size = lax.axis_size(axis)
    return swap(jnp.broadcast_to(value[None], (size,) + value.shape), axis)


def per_device(
    frames,
    lengths,
    stretch_sizes,
    look_ahead,
    norm_one,
    norm_two,
    w_query,
    w_key,
    w_value,
    w_out,
    conv_kernel,
):
    source = frames[0]
    rows, width = source.shape
    size = lax.axis_size("seq")
    place = lax.axis_index("seq").reshape(1).astype(jnp.int32)
    up = [(i, i + 1) for i in range(size - 1)]
    down = [(j, i) for i, j in up]
    before = lax.ppermute(source[rows - BEFORE :], "seq", up)
    after = lax.ppermute(source[:AFTER], "seq", down)
    taps = jnp.pad(conv_kernel.astype(F32), ((0, 1), (0, 0)))
    packed = project(source, norm_one[None], w_query, w_key, w_value)
    packed = swap(packed, "seq")
    packed, before, after = lax.optimization_barrier((packed, before, after))
    gain = norm_two[None]
    ctx = swap(attend(lengths, stretch_sizes, look_ahead, packed), "seq")
    full, near, grad = finish(place, lengths, ctx, before, source, after, w_out, gain, taps)
    piece = jnp.sum(swap(grad, "seq"), axis=0)
    piece = jnp.sum(spread_out(piece, "dp"), axis=0)
    grads = spread_out(piece, "seq")
    grads = grads.reshape(width // LANES, 32, LANES).transpose(1, 0, 2).reshape(32, width)
    return full[None], near[None], grads[:KERNEL]


def solution(mesh):
    in_specs = (P("dp", "seq", None), P("dp"), P("dp"), P("dp"), P(), P(), P(), P(), P(), P(), P())
    out_specs = (P("dp", "seq", None), P("dp", "seq", None), P())
    return jax.shard_map(
        per_device, mesh=mesh, in_specs=in_specs, out_specs=out_specs, check_vma=False
    )
```

```python
import jax
import jax.numpy as jnp
from jax import lax
from jax.experimental import pallas as pl
from jax.experimental.pallas import tpu as pltpu
from jax.sharding import PartitionSpec as P

HEADS = 16
DEPTH = 64
KERNEL = 31
LEFT = 64
EPSILON = 1e-05
FLOOR_SCORE = -1e30
BEFORE = 32
AFTER = 16
LANES = 128
TILE = 8
STRIDE = 16
PIECES = 4
QUERIES = 512
SHORTEST = 1024
F32 = jnp.float32
BF16 = jnp.bfloat16
SMEM_SPEC = pl.BlockSpec(memory_space=pltpu.SMEM)
VMEM_SPEC = pl.BlockSpec(memory_space=pltpu.VMEM)


def cost(flops, accessed):
    return pl.CostEstimate(flops=flops, bytes_accessed=accessed, transcendentals=0)


def norm_rows(values, gain):
    center = values - jnp.mean(values, axis=-1, keepdims=True)
    spread = jnp.mean(center * center, axis=-1, keepdims=True)
    return center * lax.rsqrt(spread + EPSILON) * gain


def low_lanes(rows):
    return lax.broadcasted_iota(jnp.int32, (rows, LANES), 1) < DEPTH


def half_turn(value):
    return pltpu.roll(value, DEPTH, 1)


def dot_rows(left, right):
    return lax.dot_general(left, right, (((1,), (1,)), ((), ())), preferred_element_type=F32)


def project_kernel(frames_hbm, gain_ref, wq_hbm, wk_hbm, wv_hbm, out_ref, frames_ref, w_ref, sem):
    rows, width = frames_ref.shape
    half = rows // 2
    deep = width // PIECES
    first = pltpu.make_async_copy(frames_hbm, frames_ref, sem.at[3 * PIECES])
    first.start()
    copies = []
    for index, hbm in enumerate((wk_hbm, wv_hbm, wq_hbm)):
        for piece in range(PIECES):
            span = slice(piece * deep, (piece + 1) * deep)
            copy = pltpu.make_async_copy(
                hbm.at[span], w_ref.at[index, span], sem.at[index * PIECES + piece]
            )
            copy.start()
            copies.append(copy)
    first.wait()
    normed = norm_rows(frames_ref[...].astype(F32), gain_ref[...]).astype(BF16)
    products = []
    for index in range(3):
        total = None
        for piece in range(PIECES):
            span = slice(piece * deep, (piece + 1) * deep)
            copies[index * PIECES + piece].wait()
            term = jnp.dot(normed[:, span], w_ref[index, span], preferred_element_type=F32)
            total = term if total is None else total + term
        products.append(total)
    key, value, query = products
    query = query * (DEPTH**-0.5)
    low = low_lanes(rows)
    low_half = low_lanes(half)
    for pair in range(HEADS // 2):
        cols = slice(pair * LANES, (pair + 1) * LANES)
        k, v, q = key[:, cols], value[:, cols], query[:, cols]
        kr, vr, qr = half_turn(k), half_turn(v), half_turn(q)
        out_ref[2 * pair, :rows] = jnp.where(low, k, vr).astype(BF16)
        out_ref[2 * pair + 1, :rows] = jnp.where(low, kr, v).astype(BF16)
        out_ref[2 * pair, rows:] = jnp.where(low_half, q[:half], qr[half:]).astype(BF16)
        out_ref[2 * pair + 1, rows:] = jnp.where(low_half, qr[:half], q[half:]).astype(BF16)


def project(frames, gain, wq, wk, wv):
    rows, width = frames.shape
    hbm = pl.BlockSpec(memory_space=pltpu.HBM)
    return pl.pallas_call(
        project_kernel,
        in_specs=[hbm, VMEM_SPEC, hbm, hbm, hbm],
        out_specs=VMEM_SPEC,
        out_shape=jax.ShapeDtypeStruct((HEADS, rows + rows // 2, LANES), BF16),
        scratch_shapes=[
            pltpu.VMEM((rows, width), BF16),
            pltpu.VMEM((3, width, width), BF16),
            pltpu.SemaphoreType.DMA((3 * PIECES + 1,)),
        ],
        compiler_params=pltpu.CompilerParams(vmem_limit_bytes=62 << 20),
        name="project",
    )(frames, gain, wq, wk, wv)


def row_softmax(scores):
    highest = jnp.max(scores, axis=-1, keepdims=True)
    expo = jnp.exp(scores - highest)
    return expo.astype(BF16), jnp.sum(expo, axis=-1, keepdims=True)


def attend_kernel(
    length_ref, stretch_ref, look_ref, packed_ref, before_ref, after_ref, out_ref,
    q_ref, bias_ref, s0_ref, s1_ref, full_ref, near_ref,
):
    blocks, packed_rows, _ = packed_ref.shape
    rows = packed_rows * 2 // 3
    half = rows // 2
    total = blocks * rows
    steps = total // QUERIES
    share = QUERIES // rows
    length = length_ref[0]
    length_f = length.astype(F32)
    stretch = stretch_ref[0].astype(F32)
    look = look_ref[0].astype(F32)
    low_half = low_lanes(half)
    for block in range(blocks):
        q = packed_ref[block, rows:].astype(F32)
        start = block * rows
        q_ref[start : start + half] = jnp.where(low_half, q, 0.0).astype(BF16)
        q_ref[start + half : start + rows] = jnp.where(low_half, half_turn(q), 0.0).astype(BF16)
    near_ref[:BEFORE] = jnp.zeros((BEFORE, LANES), BF16)
    full_ref[:AFTER] = jnp.zeros((AFTER, LANES), BF16)
    full_ref[AFTER + total :] = jnp.zeros((AFTER, LANES), BF16)
    key_pos = lax.broadcasted_iota(jnp.int32, (8, total), 1)
    bias_ref[...] = jnp.where(key_pos < length, 0.0, FLOOR_SCORE)
    row = lax.broadcasted_iota(jnp.int32, (rows, LANES), 0)
    lane = lax.broadcasted_iota(jnp.int32, (rows, LANES), 1)
    lane_f = lane.astype(F32)
    row_f = lax.broadcasted_iota(jnp.int32, (rows, 1), 0).astype(F32)

    def at(index):
        return pl.ds(pl.multiple_of(index * QUERIES, QUERIES), QUERIES)

    def keys(first, count):
        return jnp.concatenate([packed_ref[b, :rows] for b in range(first, first + count)], axis=0)

    def score(index, s_ref):
        q = q_ref[at(index)]
        always = SHORTEST // rows
        s_ref[:, :SHORTEST] = dot_rows(q, keys(0, always))
        s_ref[:, SHORTEST:] = dot_rows(q, keys(always, blocks - always)) + bias_ref[0:1, SHORTEST:]

    def own(index, s_ref):
        @pl.when((index + 1) * QUERIES > length)
        def _():
            for part in range(share):
                block = index * share + part
                start = pl.multiple_of(block * rows, rows)
                raw = dot_rows(q_ref[pl.ds(start, rows)], packed_ref[block, :rows])
                seen = (lane == row) | (lane + start < length)
                s_ref[part * rows : (part + 1) * rows, pl.ds(start, rows)] = jnp.where(
                    seen, raw, FLOOR_SCORE
                )

    def mix(index, s_ref):
        weights, totals = row_softmax(s_ref[...])
        mixed = jnp.dot(weights, keys(0, blocks), preferred_element_type=F32)
        full_ref[pl.ds(pl.multiple_of(index * QUERIES + AFTER, AFTER), QUERIES)] = half_turn(
            mixed / totals
        ).astype(BF16)

    def near(block):
        start = pl.multiple_of(block * rows, rows)
        base = (block * rows).astype(F32) if not isinstance(block, int) else float(block * rows)
        pos = row_f + base
        begin = jnp.floor((pos + 0.5) / stretch) * stretch
        first = jnp.broadcast_to(jnp.maximum(begin - LEFT, 0.0) - base, (rows, LANES))
        last = jnp.broadcast_to(jnp.minimum(begin + stretch + look, length_f) - base, (rows, LANES))
        around = (jnp.maximum(block - 1, 0), block, jnp.minimum(block + 1, blocks - 1))
        window = jnp.concatenate([packed_ref[b, :rows] for b in around], axis=0)
        raw = dot_rows(q_ref[pl.ds(start, rows)], window)
        parts = []
        for part in range(3):
            key_at = lane_f + float((part - 1) * rows)
            inside = (key_at >= first) & (key_at < last)
            if part == 1:
                inside = inside | (lane == row)
            parts.append(jnp.where(inside, raw[:, part * rows : (part + 1) * rows], FLOOR_SCORE))
        weights, totals = row_softmax(jnp.concatenate(parts, axis=1))
        mixed = jnp.dot(weights, window, preferred_element_type=F32)
        near_ref[pl.ds(pl.multiple_of(start + BEFORE, BEFORE), rows)] = (mixed / totals).astype(
            BF16
        )

    def nears(index):
        for part in range(share):
            near(index * share + part)

    score(0, s0_ref)
    own(0, s0_ref)

    def body(step, carry):
        score(2 * step + 1, s1_ref)
        mix(2 * step, s0_ref)
        nears(2 * step)
        own(2 * step + 1, s1_ref)
        score(2 * step + 2, s0_ref)
        mix(2 * step + 1, s1_ref)
        nears(2 * step + 1)
        own(2 * step + 2, s0_ref)
        return carry

    lax.fori_loop(0, steps // 2 - 1, body, 0)
    score(steps - 1, s1_ref)
    mix(steps - 2, s0_ref)
    nears(jnp.int32(steps - 2))
    own(steps - 1, s1_ref)
    mix(steps - 1, s1_ref)
    nears(jnp.int32(steps - 1))
    ext = BEFORE + rows
    low = low_lanes(ext)
    for block in range(blocks):
        span = slice(block * rows, block * rows + ext)
        out_ref[block] = jnp.where(
            low, full_ref[span].astype(F32), near_ref[span].astype(F32)
        ).astype(BF16)


def attend(length, stretch, look, packed, before, after):
    blocks, packed_rows, _ = packed.shape
    rows = packed_rows * 2 // 3
    total = blocks * rows
    return pl.pallas_call(
        attend_kernel,
        in_specs=[SMEM_SPEC] * 3 + [VMEM_SPEC] + [pl.BlockSpec(memory_space=pl.ANY)] * 2,
        out_specs=VMEM_SPEC,
        out_shape=jax.ShapeDtypeStruct((blocks, BEFORE + rows, LANES), BF16),
        scratch_shapes=[
            pltpu.VMEM((total, LANES), BF16),
            pltpu.VMEM((8, total), F32),
            pltpu.VMEM((QUERIES, total), F32),
            pltpu.VMEM((QUERIES, total), F32),
            pltpu.VMEM((total + 2 * AFTER, LANES), BF16),
            pltpu.VMEM((BEFORE + total, LANES), BF16),
        ],
        compiler_params=pltpu.CompilerParams(vmem_limit_bytes=32 << 20),
        name="attend",
    )(length, stretch, look, packed, before, after)


def frame_tile(ref, index):
    return ref[pl.ds(pl.multiple_of(index * TILE, TILE), TILE), :]


def cells(first, tile):
    return pl.ds(first * TILE + tile, TILE, stride=TILE)


def convolve(x_ref, taps, first):
    totals = [None] * STRIDE
    for step in range(STRIDE + KERNEL - 1):
        x = frame_tile(x_ref, first + step)
        for row in range(max(0, step - KERNEL + 1), min(STRIDE, step + 1)):
            term = taps[step - row] * x
            totals[row] = term if totals[row] is None else totals[row] + term
    return totals


def finish_kernel(
    place_ref, length_ref, ctx_ref, before_ref, frames_ref, after_ref, wo_ref, gain_ref, taps_ref,
    full_ref, near_ref, grad_ref,
    c_ref, res_ref, xf_ref, xn_ref, cf_ref, cn_ref, slope_ref, sums_ref,
):
    rows, width = frames_ref.shape
    ext = BEFORE + rows
    length = length_ref[0]
    start = place_ref[0] * rows
    low = low_lanes(ext)
    for pair in range(HEADS // 2):
        cols = slice(pair * LANES, (pair + 1) * LANES)
        one, two = ctx_ref[2 * pair].astype(F32), ctx_ref[2 * pair + 1].astype(F32)
        c_ref[:ext, cols] = jnp.where(low, one, half_turn(two)).astype(BF16)
        c_ref[ext:, cols] = jnp.where(low, half_turn(one), two).astype(BF16)
    frames = frames_ref[...]
    source = jnp.concatenate(
        [before_ref[BEFORE - AFTER :], frames, after_ref[...], before_ref[...], frames], axis=0
    ).astype(F32)
    residual = source + jnp.dot(c_ref[...], wo_ref[...], preferred_element_type=F32)
    res_ref[...] = residual
    normed = norm_rows(residual, gain_ref[...])
    line = lax.broadcasted_iota(jnp.int32, (2 * ext, 1), 0)
    pos = start + jnp.where(line < ext, line - AFTER, line - ext - BEFORE)
    valid = (pos >= 0) & (pos < length)
    x = jnp.where(valid, normed, 0.0).astype(BF16).astype(F32)
    for x_ref, at in ((xf_ref, 0), (xn_ref, ext)):
        for first in range(0, ext, TILE):
            for tile in range(width // LANES):
                x_ref[cells(first, tile), :] = x[
                    at + first : at + first + TILE, tile * LANES : (tile + 1) * LANES
                ]
    full_first = AFTER - KERNEL // 2
    near_first = BEFORE - (KERNEL - 1)

    def conv_rows(step, carry):
        taps = [frame_tile(taps_ref, k) for k in range(KERNEL)]
        at = step * STRIDE
        for x_ref, first, out_ref in ((xf_ref, full_first, cf_ref), (xn_ref, near_first, cn_ref)):
            for row, value in enumerate(convolve(x_ref, taps, at + first)):
                out_ref[pl.ds(pl.multiple_of((at + row) * TILE, TILE), TILE), :] = value
        return carry

    lax.fori_loop(0, rows // STRIDE, conv_rows, 0)
    inner = lax.broadcasted_iota(jnp.int32, (rows, 1), 0) + start
    factor = jnp.where(inner < length, 2.0 / jnp.sqrt(jnp.full((rows, 1), length.astype(F32))), 0.0)
    for tile in range(width // LANES):
        cols = slice(tile * LANES, (tile + 1) * LANES)
        groups = range(0, rows, TILE)
        conv = jnp.concatenate([cf_ref[cells(g, tile), :] for g in groups], axis=0)
        out_full = res_ref[AFTER : AFTER + rows, cols] + conv / (1.0 + jnp.exp(-conv))
        full_ref[:, cols] = out_full.astype(BF16)
        conv = jnp.concatenate([cn_ref[cells(g, tile), :] for g in groups], axis=0)
        sigma = 1.0 / (1.0 + jnp.exp(-conv))
        out_near = res_ref[ext + BEFORE :, cols] + conv * sigma
        near_ref[:, cols] = out_near.astype(BF16)
        slope = (out_near - out_full) * factor * (sigma * (1.0 + conv * (1.0 - sigma)))
        for g in groups:
            slope_ref[cells(g, tile), :] = slope[g : g + TILE]

    def grad_rows(step, sums):
        sums = list(sums)
        at = step * STRIDE
        slopes = [frame_tile(slope_ref, at + row) for row in range(STRIDE)]
        for move in range(STRIDE + KERNEL - 1):
            x = frame_tile(xn_ref, at + near_first + move)
            for row in range(max(0, move - KERNEL + 1), min(STRIDE, move + 1)):
                sums[move - row] = sums[move - row] + slopes[row] * x
        return tuple(sums)

    zero = jnp.zeros((TILE, LANES), F32)
    sums = lax.fori_loop(0, rows // STRIDE, grad_rows, (zero,) * KERNEL)
    for k, value in enumerate(sums + (zero,)):
        sums_ref[k * TILE : (k + 1) * TILE] = value
    for tile in range(width // LANES):
        for group in range(4):
            grad_ref[2 * tile + group // 2, group % 2 * TILE : group % 2 * TILE + TILE] = sums_ref[
                cells(group * TILE, tile), :
            ]


def finish(place, length, ctx, before, frames, after, wo, gain, taps):
    rows, width = frames.shape
    ext = BEFORE + rows
    return pl.pallas_call(
        finish_kernel,
        in_specs=[SMEM_SPEC] * 2 + [VMEM_SPEC] * 7,
        out_specs=[VMEM_SPEC] * 3,
        out_shape=[
            jax.ShapeDtypeStruct((rows, width), BF16),
            jax.ShapeDtypeStruct((rows, width), BF16),
            jax.ShapeDtypeStruct((width // 64, 16, LANES), F32),
        ],
        scratch_shapes=[
            pltpu.VMEM((2 * ext, width), BF16),
            pltpu.VMEM((2 * ext, width), F32),
            pltpu.VMEM((ext * TILE, LANES), F32),
            pltpu.VMEM((ext * TILE, LANES), F32),
            pltpu.VMEM((rows * TILE, LANES), F32),
            pltpu.VMEM((rows * TILE, LANES), F32),
            pltpu.VMEM((rows * TILE, LANES), F32),
            pltpu.VMEM((32 * TILE, LANES), F32),
        ],
        compiler_params=pltpu.CompilerParams(vmem_limit_bytes=40 << 20),
        name="finish",
    )(place, length, ctx, before, frames, after, wo, gain, taps)


def swap(value, axis):
    return lax.all_to_all(value, axis, 0, 0, tiled=True)


def spread_out(value, axis):
    size = lax.axis_size(axis)
    return swap(jnp.broadcast_to(value[None], (size,) + value.shape), axis)


def per_device(
    frames,
    lengths,
    stretch_sizes,
    look_ahead,
    norm_one,
    norm_two,
    w_query,
    w_key,
    w_value,
    w_out,
    conv_kernel,
):
    source = frames[0]
    rows, width = source.shape
    size = lax.axis_size("seq")
    place = lax.axis_index("seq").reshape(1).astype(jnp.int32)
    up = [(i, i + 1) for i in range(size - 1)]
    down = [(j, i) for i, j in up]
    before = lax.ppermute(source[rows - BEFORE :], "seq", up)
    after = lax.ppermute(source[:AFTER], "seq", down)
    taps = conv_kernel.astype(F32).reshape(KERNEL * TILE, LANES)
    packed = project(source, norm_one[None], w_query, w_key, w_value)
    packed = swap(packed, "seq")
    gain = norm_two[None]
    ctx = swap(attend(lengths, stretch_sizes, look_ahead, packed, before, after), "seq")
    full, near, grad = finish(place, lengths, ctx, before, source, after, w_out, gain, taps)
    piece = jnp.sum(swap(grad, "seq"), axis=0)
    piece = jnp.sum(spread_out(piece, "dp"), axis=0)
    grads = spread_out(piece, "seq")
    grads = grads.reshape(width // LANES, 32, LANES).transpose(1, 0, 2).reshape(32, width)
    return full[None], near[None], grads[:KERNEL]


def solution(mesh):
    in_specs = (P("dp", "seq", None), P("dp"), P("dp"), P("dp"), P(), P(), P(), P(), P(), P(), P())
    out_specs = (P("dp", "seq", None), P("dp", "seq", None), P())
    return jax.shard_map(
        per_device, mesh=mesh, in_specs=in_specs, out_specs=out_specs, check_vma=False
    )
```

```python
import jax
import jax.numpy as jnp
from jax import lax
from jax.experimental import pallas as pl
from jax.experimental.pallas import tpu as pltpu
from jax.sharding import PartitionSpec as P

HEADS = 16
DEPTH = 64
KERNEL = 31
LEFT = 64
EPSILON = 1e-05
FLOOR_SCORE = -1e30
BEFORE = 32
AFTER = 16
LANES = 128
TILE = 8
STRIDE = 16
PIECES = 4
QUERIES = 512
SHORTEST = 1024
F32 = jnp.float32
BF16 = jnp.bfloat16
SMEM_SPEC = pl.BlockSpec(memory_space=pltpu.SMEM)
VMEM_SPEC = pl.BlockSpec(memory_space=pltpu.VMEM)


def cost(flops, accessed):
    return pl.CostEstimate(flops=flops, bytes_accessed=accessed, transcendentals=0)


def norm_rows(values, gain):
    center = values - jnp.mean(values, axis=-1, keepdims=True)
    spread = jnp.mean(center * center, axis=-1, keepdims=True)
    return center * lax.rsqrt(spread + EPSILON) * gain


def low_lanes(rows):
    return lax.broadcasted_iota(jnp.int32, (rows, LANES), 1) < DEPTH


def half_turn(value):
    return pltpu.roll(value, DEPTH, 1)


def dot_rows(left, right):
    return lax.dot_general(left, right, (((1,), (1,)), ((), ())), preferred_element_type=F32)


def project_kernel(frames_hbm, gain_ref, wq_hbm, wk_hbm, wv_hbm, out_ref, frames_ref, w_ref, sem):
    rows, width = frames_ref.shape
    half = rows // 2
    deep = width // PIECES
    first = pltpu.make_async_copy(frames_hbm, frames_ref, sem.at[3 * PIECES])
    first.start()
    copies = []
    for index, hbm in enumerate((wk_hbm, wv_hbm, wq_hbm)):
        for piece in range(PIECES):
            span = slice(piece * deep, (piece + 1) * deep)
            copy = pltpu.make_async_copy(
                hbm.at[span], w_ref.at[index, span], sem.at[index * PIECES + piece]
            )
            copy.start()
            copies.append(copy)
    first.wait()
    normed = norm_rows(frames_ref[...].astype(F32), gain_ref[...]).astype(BF16)
    products = []
    for index in range(3):
        total = None
        for piece in range(PIECES):
            span = slice(piece * deep, (piece + 1) * deep)
            copies[index * PIECES + piece].wait()
            term = jnp.dot(normed[:, span], w_ref[index, span], preferred_element_type=F32)
            total = term if total is None else total + term
        products.append(total)
    key, value, query = products
    query = query * (DEPTH**-0.5)
    low = low_lanes(rows)
    low_half = low_lanes(half)
    for pair in range(HEADS // 2):
        cols = slice(pair * LANES, (pair + 1) * LANES)
        k, v, q = key[:, cols], value[:, cols], query[:, cols]
        kr, vr, qr = half_turn(k), half_turn(v), half_turn(q)
        out_ref[2 * pair, :rows] = jnp.where(low, k, vr).astype(BF16)
        out_ref[2 * pair + 1, :rows] = jnp.where(low, kr, v).astype(BF16)
        out_ref[2 * pair, rows:] = jnp.where(low_half, q[:half], qr[half:]).astype(BF16)
        out_ref[2 * pair + 1, rows:] = jnp.where(low_half, qr[:half], q[half:]).astype(BF16)


def project(frames, gain, wq, wk, wv):
    rows, width = frames.shape
    hbm = pl.BlockSpec(memory_space=pltpu.HBM)
    return pl.pallas_call(
        project_kernel,
        in_specs=[hbm, VMEM_SPEC, hbm, hbm, hbm],
        out_specs=VMEM_SPEC,
        out_shape=jax.ShapeDtypeStruct((HEADS, rows + rows // 2, LANES), BF16),
        scratch_shapes=[
            pltpu.VMEM((rows, width), BF16),
            pltpu.VMEM((3, width, width), BF16),
            pltpu.SemaphoreType.DMA((3 * PIECES + 1,)),
        ],
        compiler_params=pltpu.CompilerParams(vmem_limit_bytes=62 << 20),
        name="project",
    )(frames, gain, wq, wk, wv)


def row_softmax(scores):
    highest = jnp.max(scores, axis=-1, keepdims=True)
    expo = jnp.exp(scores - highest)
    return expo.astype(BF16), jnp.sum(expo, axis=-1, keepdims=True)


def attend_kernel(
    length_ref, stretch_ref, look_ref, packed_ref, before_ref, after_ref, out_ref,
    q_ref, bias_ref, s0_ref, s1_ref, w_ref, full_ref, near_ref,
):
    blocks, packed_rows, _ = packed_ref.shape
    rows = packed_rows * 2 // 3
    half = rows // 2
    total = blocks * rows
    steps = total // QUERIES
    share = QUERIES // rows
    length = length_ref[0]
    stretch = stretch_ref[0].astype(F32)
    look = look_ref[0].astype(F32)
    low_half = low_lanes(half)
    for block in range(blocks):
        q = packed_ref[block, rows:].astype(F32)
        start = block * rows
        q_ref[start : start + half] = jnp.where(low_half, q, 0.0).astype(BF16)
        q_ref[start + half : start + rows] = jnp.where(low_half, half_turn(q), 0.0).astype(BF16)
    w_ref[...] = jnp.zeros_like(w_ref)
    near_ref[:BEFORE] = jnp.zeros((BEFORE, LANES), BF16)
    full_ref[:AFTER] = jnp.zeros((AFTER, LANES), BF16)
    full_ref[AFTER + total :] = jnp.zeros((AFTER, LANES), BF16)
    key_pos = lax.broadcasted_iota(jnp.int32, (8, total), 1)
    bias_ref[...] = jnp.where(key_pos < length, 0.0, FLOOR_SCORE)
    row = lax.broadcasted_iota(jnp.int32, (rows, LANES), 0)
    lane = lax.broadcasted_iota(jnp.int32, (rows, LANES), 1)
    lane_f = lane.astype(F32)
    row_f = lax.broadcasted_iota(jnp.int32, (rows, 1), 0).astype(F32)

    def at(index):
        return pl.ds(pl.multiple_of(index * QUERIES, QUERIES), QUERIES)

    def keys(first, count):
        return jnp.concatenate([packed_ref[b, :rows] for b in range(first, first + count)], axis=0)

    def score(index, s_ref):
        q = q_ref[at(index)]
        top = None
        for first in range(0, total, 512):
            cols = slice(first, first + 512)
            part = dot_rows(q, keys(first // rows, 512 // rows))
            if first >= SHORTEST:
                part = part + bias_ref[0:1, cols]
            s_ref[:, cols] = part
            for lane_at in range(0, 512, LANES):
                piece = part[:, lane_at : lane_at + LANES]
                top = piece if top is None else jnp.maximum(top, piece)
        s_ref[:, total:] = top

    def own(index, s_ref):
        @pl.when((index + 1) * QUERIES > length)
        def _():
            for part in range(share):
                block = index * share + part
                start = pl.multiple_of(block * rows, rows)
                raw = dot_rows(q_ref[pl.ds(start, rows)], packed_ref[block, :rows])
                seen = (lane == row) | (lane + start < length)
                raw = jnp.where(seen, raw, FLOOR_SCORE)
                span = slice(part * rows, (part + 1) * rows)
                s_ref[span, pl.ds(start, rows)] = raw
                s_ref[span, total:] = jnp.maximum(s_ref[span, total:], raw)

    def mix(index, s_ref):
        highest = jnp.max(s_ref[:, total:], axis=-1, keepdims=True)
        expo = jnp.exp(s_ref[:, :total] - highest)
        totals = jnp.sum(expo, axis=-1, keepdims=True)
        weights = expo.astype(BF16)
        mixed = jnp.dot(weights, keys(0, blocks), preferred_element_type=F32)
        full_ref[pl.ds(pl.multiple_of(index * QUERIES + AFTER, AFTER), QUERIES)] = half_turn(
            mixed / totals
        ).astype(BF16)

    def near(index, s_ref):
        sums = []
        for part in range(share):
            block = index * share + part
            base = (block * rows).astype(F32)
            begin = jnp.floor((row_f + base + 0.5) / stretch) * stretch
            first = jnp.broadcast_to(jnp.maximum(begin - LEFT, 0.0) - base, (rows, LANES))
            last = jnp.broadcast_to(
                jnp.minimum(begin + stretch + look, float(total)) - base, (rows, LANES)
            )
            span = slice(part * rows, (part + 1) * rows)
            around = (jnp.maximum(block - 1, 0), block, jnp.minimum(block + 1, blocks - 1))
            pieces = []
            for place, other in enumerate(around):
                key_at = lane_f + float((place - 1) * rows)
                if place == 0:
                    inside = key_at >= first
                elif place == 1:
                    inside = (key_at >= first) & (key_at < last)
                else:
                    inside = key_at < last
                raw = s_ref[span, pl.ds(pl.multiple_of(other * rows, rows), rows)]
                pieces.append(jnp.where(inside, raw, FLOOR_SCORE))
            weights, totals = row_softmax(jnp.concatenate(pieces, axis=1))
            w_ref[span, part * rows : (part + 3) * rows] = weights
            sums.append(totals)
        others = [jnp.clip(index * share + b, 0, blocks - 1) for b in range(-1, share + 1)]
        window = jnp.concatenate([packed_ref[b, :rows] for b in others], axis=0)
        mixed = jnp.dot(w_ref[...], window, preferred_element_type=F32)
        near_ref[pl.ds(pl.multiple_of(index * QUERIES + BEFORE, BEFORE), QUERIES)] = (
            mixed / jnp.concatenate(sums, axis=0)
        ).astype(BF16)

    score(0, s0_ref)
    own(0, s0_ref)

    def body(step, carry):
        score(2 * step + 1, s1_ref)
        mix(2 * step, s0_ref)
        near(2 * step, s0_ref)
        own(2 * step + 1, s1_ref)
        score(2 * step + 2, s0_ref)
        mix(2 * step + 1, s1_ref)
        near(2 * step + 1, s1_ref)
        own(2 * step + 2, s0_ref)
        return carry

    lax.fori_loop(0, steps // 2 - 1, body, 0)
    score(steps - 1, s1_ref)
    mix(steps - 2, s0_ref)
    near(jnp.int32(steps - 2), s0_ref)
    own(steps - 1, s1_ref)
    mix(steps - 1, s1_ref)
    near(jnp.int32(steps - 1), s1_ref)
    ext = BEFORE + rows
    low = low_lanes(ext)
    for block in range(blocks):
        span = slice(block * rows, block * rows + ext)
        out_ref[block] = jnp.where(low, full_ref[span], near_ref[span])


def attend(length, stretch, look, packed, before, after):
    blocks, packed_rows, _ = packed.shape
    rows = packed_rows * 2 // 3
    total = blocks * rows
    return pl.pallas_call(
        attend_kernel,
        in_specs=[SMEM_SPEC] * 3 + [VMEM_SPEC] + [pl.BlockSpec(memory_space=pl.ANY)] * 2,
        out_specs=VMEM_SPEC,
        out_shape=jax.ShapeDtypeStruct((blocks, BEFORE + rows, LANES), BF16),
        scratch_shapes=[
            pltpu.VMEM((total, LANES), BF16),
            pltpu.VMEM((8, total), F32),
            pltpu.VMEM((QUERIES, total + LANES), F32),
            pltpu.VMEM((QUERIES, total + LANES), F32),
            pltpu.VMEM((QUERIES, QUERIES + 2 * rows), BF16),
            pltpu.VMEM((total + 2 * AFTER, LANES), BF16),
            pltpu.VMEM((BEFORE + total, LANES), BF16),
        ],
        compiler_params=pltpu.CompilerParams(vmem_limit_bytes=32 << 20),
        name="attend",
    )(length, stretch, look, packed, before, after)


def frame_tile(ref, index):
    return ref[pl.ds(pl.multiple_of(index * TILE, TILE), TILE), :]


def cells(first, tile):
    return pl.ds(first * TILE + tile, TILE, stride=TILE)


def convolve(x_ref, taps, first):
    totals = [None] * STRIDE
    for step in range(STRIDE + KERNEL - 1):
        x = frame_tile(x_ref, first + step)
        for row in range(max(0, step - KERNEL + 1), min(STRIDE, step + 1)):
            term = taps[step - row] * x
            totals[row] = term if totals[row] is None else totals[row] + term
    return totals


def finish_kernel(
    place_ref, length_ref, ctx_ref, before_ref, frames_ref, after_ref, wo_ref, gain_ref, taps_ref,
    full_ref, near_ref, grad_ref,
    c_ref, res_ref, xf_ref, xn_ref, cf_ref, cn_ref, slope_ref, sums_ref,
):
    rows, width = frames_ref.shape
    ext = BEFORE + rows
    length = length_ref[0]
    start = place_ref[0] * rows
    low = low_lanes(ext)
    for pair in range(HEADS // 2):
        cols = slice(pair * LANES, (pair + 1) * LANES)
        one, two = ctx_ref[2 * pair].astype(F32), ctx_ref[2 * pair + 1].astype(F32)
        c_ref[:ext, cols] = jnp.where(low, one, half_turn(two)).astype(BF16)
        c_ref[ext:, cols] = jnp.where(low, half_turn(one), two).astype(BF16)
    frames = frames_ref[...]
    source = jnp.concatenate(
        [before_ref[BEFORE - AFTER :], frames, after_ref[...], before_ref[...], frames], axis=0
    ).astype(F32)
    residual = source + jnp.dot(c_ref[...], wo_ref[...], preferred_element_type=F32)
    res_ref[...] = residual
    normed = norm_rows(residual, gain_ref[...])
    line = lax.broadcasted_iota(jnp.int32, (2 * ext, 1), 0)
    pos = start + jnp.where(line < ext, line - AFTER, line - ext - BEFORE)
    valid = (pos >= 0) & (pos < length)
    x = jnp.where(valid, normed, 0.0).astype(BF16).astype(F32)
    for x_ref, at in ((xf_ref, 0), (xn_ref, ext)):
        for first in range(0, ext, TILE):
            for tile in range(width // LANES):
                x_ref[cells(first, tile), :] = x[
                    at + first : at + first + TILE, tile * LANES : (tile + 1) * LANES
                ]
    full_first = AFTER - KERNEL // 2
    near_first = BEFORE - (KERNEL - 1)

    def conv_rows(step, carry):
        taps = [frame_tile(taps_ref, k) for k in range(KERNEL)]
        at = step * STRIDE
        for x_ref, first, out_ref in ((xf_ref, full_first, cf_ref), (xn_ref, near_first, cn_ref)):
            for row, value in enumerate(convolve(x_ref, taps, at + first)):
                out_ref[pl.ds(pl.multiple_of((at + row) * TILE, TILE), TILE), :] = value
        return carry

    lax.fori_loop(0, rows // STRIDE, conv_rows, 0)
    inner = lax.broadcasted_iota(jnp.int32, (rows, 1), 0) + start
    factor = jnp.where(inner < length, 2.0 / jnp.sqrt(jnp.full((rows, 1), length.astype(F32))), 0.0)
    for tile in range(width // LANES):
        cols = slice(tile * LANES, (tile + 1) * LANES)
        groups = range(0, rows, TILE)
        conv = jnp.concatenate([cf_ref[cells(g, tile), :] for g in groups], axis=0)
        out_full = res_ref[AFTER : AFTER + rows, cols] + conv / (1.0 + jnp.exp(-conv))
        full_ref[:, cols] = out_full.astype(BF16)
        conv = jnp.concatenate([cn_ref[cells(g, tile), :] for g in groups], axis=0)
        sigma = 1.0 / (1.0 + jnp.exp(-conv))
        out_near = res_ref[ext + BEFORE :, cols] + conv * sigma
        near_ref[:, cols] = out_near.astype(BF16)
        slope = (out_near - out_full) * factor * (sigma * (1.0 + conv * (1.0 - sigma)))
        for g in groups:
            slope_ref[cells(g, tile), :] = slope[g : g + TILE]

    def grad_rows(step, sums):
        sums = list(sums)
        at = step * STRIDE
        slopes = [frame_tile(slope_ref, at + row) for row in range(STRIDE)]
        for move in range(STRIDE + KERNEL - 1):
            x = frame_tile(xn_ref, at + near_first + move)
            for row in range(max(0, move - KERNEL + 1), min(STRIDE, move + 1)):
                sums[move - row] = sums[move - row] + slopes[row] * x
        return tuple(sums)

    zero = jnp.zeros((TILE, LANES), F32)
    sums = lax.fori_loop(0, rows // STRIDE, grad_rows, (zero,) * KERNEL)
    for k, value in enumerate(sums + (zero,)):
        sums_ref[k * TILE : (k + 1) * TILE] = value
    for tile in range(width // LANES):
        for group in range(4):
            grad_ref[2 * tile + group // 2, group % 2 * TILE : group % 2 * TILE + TILE] = sums_ref[
                cells(group * TILE, tile), :
            ]


def finish(place, length, ctx, before, frames, after, wo, gain, taps):
    rows, width = frames.shape
    ext = BEFORE + rows
    return pl.pallas_call(
        finish_kernel,
        in_specs=[SMEM_SPEC] * 2 + [VMEM_SPEC] * 7,
        out_specs=[VMEM_SPEC] * 3,
        out_shape=[
            jax.ShapeDtypeStruct((rows, width), BF16),
            jax.ShapeDtypeStruct((rows, width), BF16),
            jax.ShapeDtypeStruct((width // 64, 16, LANES), F32),
        ],
        scratch_shapes=[
            pltpu.VMEM((2 * ext, width), BF16),
            pltpu.VMEM((2 * ext, width), F32),
            pltpu.VMEM((ext * TILE, LANES), F32),
            pltpu.VMEM((ext * TILE, LANES), F32),
            pltpu.VMEM((rows * TILE, LANES), F32),
            pltpu.VMEM((rows * TILE, LANES), F32),
            pltpu.VMEM((rows * TILE, LANES), F32),
            pltpu.VMEM((32 * TILE, LANES), F32),
        ],
        compiler_params=pltpu.CompilerParams(vmem_limit_bytes=40 << 20),
        name="finish",
    )(place, length, ctx, before, frames, after, wo, gain, taps)


def swap(value, axis):
    return lax.all_to_all(value, axis, 0, 0, tiled=True)


def spread_out(value, axis):
    size = lax.axis_size(axis)
    return swap(jnp.broadcast_to(value[None], (size,) + value.shape), axis)


def per_device(
    frames,
    lengths,
    stretch_sizes,
    look_ahead,
    norm_one,
    norm_two,
    w_query,
    w_key,
    w_value,
    w_out,
    conv_kernel,
):
    source = frames[0]
    rows, width = source.shape
    size = lax.axis_size("seq")
    place = lax.axis_index("seq").reshape(1).astype(jnp.int32)
    up = [(i, i + 1) for i in range(size - 1)]
    down = [(j, i) for i, j in up]
    before = lax.ppermute(source[rows - BEFORE :], "seq", up)
    after = lax.ppermute(source[:AFTER], "seq", down)
    taps = conv_kernel.astype(F32).reshape(KERNEL * TILE, LANES)
    packed = project(source, norm_one[None], w_query, w_key, w_value)
    packed = swap(packed, "seq")
    gain = norm_two[None]
    ctx = swap(attend(lengths, stretch_sizes, look_ahead, packed, before, after), "seq")
    full, near, grad = finish(place, lengths, ctx, before, source, after, w_out, gain, taps)
    piece = jnp.sum(swap(grad, "seq"), axis=0)
    piece = jnp.sum(spread_out(piece, "dp"), axis=0)
    grads = spread_out(piece, "seq")
    grads = grads.reshape(width // LANES, 32, LANES).transpose(1, 0, 2).reshape(32, width)
    return full[None], near[None], grads[:KERNEL]


def solution(mesh):
    in_specs = (P("dp", "seq", None), P("dp"), P("dp"), P("dp"), P(), P(), P(), P(), P(), P(), P())
    out_specs = (P("dp", "seq", None), P("dp", "seq", None), P())
    return jax.shard_map(
        per_device, mesh=mesh, in_specs=in_specs, out_specs=out_specs, check_vma=False
    )
```

```python
import jax
import jax.numpy as jnp
from jax import lax
from jax.experimental import pallas as pl
from jax.experimental.pallas import tpu as pltpu
from jax.sharding import PartitionSpec as P

HEADS = 16
DEPTH = 64
KERNEL = 31
LEFT = 64
EPSILON = 1e-05
FLOOR_SCORE = -1e30
BEFORE = 32
AFTER = 16
LANES = 128
TILE = 8
STRIDE = 16
PIECES = 4
QUERIES = 512
SHORTEST = 1024
F32 = jnp.float32
BF16 = jnp.bfloat16
SMEM_SPEC = pl.BlockSpec(memory_space=pltpu.SMEM)
VMEM_SPEC = pl.BlockSpec(memory_space=pltpu.VMEM)


def cost(flops, accessed):
    return pl.CostEstimate(flops=flops, bytes_accessed=accessed, transcendentals=0)


def norm_rows(values, gain):
    center = values - jnp.mean(values, axis=-1, keepdims=True)
    spread = jnp.mean(center * center, axis=-1, keepdims=True)
    return center * lax.rsqrt(spread + EPSILON) * gain


def low_lanes(rows):
    return lax.broadcasted_iota(jnp.int32, (rows, LANES), 1) < DEPTH


def half_turn(value):
    return pltpu.roll(value, DEPTH, 1)


def dot_rows(left, right):
    return lax.dot_general(left, right, (((1,), (1,)), ((), ())), preferred_element_type=F32)


def project_kernel(frames_hbm, gain_ref, wq_hbm, wk_hbm, wv_hbm, out_ref, frames_ref, w_ref, sem):
    rows, width = frames_ref.shape
    half = rows // 2
    deep = width // PIECES
    first = pltpu.make_async_copy(frames_hbm, frames_ref, sem.at[3 * PIECES])
    first.start()
    copies = []
    for index, hbm in enumerate((wk_hbm, wv_hbm, wq_hbm)):
        for piece in range(PIECES):
            span = slice(piece * deep, (piece + 1) * deep)
            copy = pltpu.make_async_copy(
                hbm.at[span], w_ref.at[index, span], sem.at[index * PIECES + piece]
            )
            copy.start()
            copies.append(copy)
    first.wait()
    normed = norm_rows(frames_ref[...].astype(F32), gain_ref[...]).astype(BF16)
    products = []
    for index in range(3):
        total = None
        for piece in range(PIECES):
            span = slice(piece * deep, (piece + 1) * deep)
            copies[index * PIECES + piece].wait()
            term = jnp.dot(normed[:, span], w_ref[index, span], preferred_element_type=F32)
            total = term if total is None else total + term
        products.append(total)
    key, value, query = products
    query = query * (DEPTH**-0.5)
    low = low_lanes(rows)
    low_half = low_lanes(half)
    for pair in range(HEADS // 2):
        cols = slice(pair * LANES, (pair + 1) * LANES)
        k, v, q = key[:, cols], value[:, cols], query[:, cols]
        kr, vr, qr = half_turn(k), half_turn(v), half_turn(q)
        out_ref[2 * pair, :rows] = jnp.where(low, k, vr).astype(BF16)
        out_ref[2 * pair + 1, :rows] = jnp.where(low, kr, v).astype(BF16)
        out_ref[2 * pair, rows:] = jnp.where(low_half, q[:half], qr[half:]).astype(BF16)
        out_ref[2 * pair + 1, rows:] = jnp.where(low_half, qr[:half], q[half:]).astype(BF16)


def project(frames, gain, wq, wk, wv):
    rows, width = frames.shape
    hbm = pl.BlockSpec(memory_space=pltpu.HBM)
    return pl.pallas_call(
        project_kernel,
        in_specs=[hbm, VMEM_SPEC, hbm, hbm, hbm],
        out_specs=VMEM_SPEC,
        out_shape=jax.ShapeDtypeStruct((HEADS, rows + rows // 2, LANES), BF16),
        scratch_shapes=[
            pltpu.VMEM((rows, width), BF16),
            pltpu.VMEM((3, width, width), BF16),
            pltpu.SemaphoreType.DMA((3 * PIECES + 1,)),
        ],
        compiler_params=pltpu.CompilerParams(vmem_limit_bytes=62 << 20),
        name="project",
    )(frames, gain, wq, wk, wv)


def row_softmax(scores):
    highest = jnp.max(scores, axis=-1, keepdims=True)
    expo = jnp.exp(scores - highest)
    return expo.astype(BF16), jnp.sum(expo, axis=-1, keepdims=True)


def attend_kernel(
    length_ref, stretch_ref, look_ref, packed_ref, before_ref, after_ref, out_ref,
    q_ref, bias_ref, s0_ref, s1_ref, w_ref, full_ref, near_ref,
):
    blocks, packed_rows, _ = packed_ref.shape
    rows = packed_rows * 2 // 3
    half = rows // 2
    total = blocks * rows
    steps = total // QUERIES
    share = QUERIES // rows
    length = length_ref[0]
    stretch = stretch_ref[0].astype(F32)
    look = look_ref[0].astype(F32)
    low_half = low_lanes(half)
    for block in range(blocks):
        q = packed_ref[block, rows:].astype(F32)
        start = block * rows
        q_ref[start : start + half] = jnp.where(low_half, q, 0.0).astype(BF16)
        q_ref[start + half : start + rows] = jnp.where(low_half, half_turn(q), 0.0).astype(BF16)
    w_ref[...] = jnp.zeros_like(w_ref)
    near_ref[:BEFORE] = jnp.zeros((BEFORE, LANES), BF16)
    full_ref[:AFTER] = jnp.zeros((AFTER, LANES), BF16)
    full_ref[AFTER + total :] = jnp.zeros((AFTER, LANES), BF16)
    key_pos = lax.broadcasted_iota(jnp.int32, (8, total), 1)
    bias_ref[...] = jnp.where(key_pos < length, 0.0, FLOOR_SCORE)
    row = lax.broadcasted_iota(jnp.int32, (rows, LANES), 0)
    lane = lax.broadcasted_iota(jnp.int32, (rows, LANES), 1)
    lane_f = lane.astype(F32)
    row_f = lax.broadcasted_iota(jnp.int32, (rows, 1), 0).astype(F32)

    def at(index):
        return pl.ds(pl.multiple_of(index * QUERIES, QUERIES), QUERIES)

    def keys(first, count):
        return jnp.concatenate([packed_ref[b, :rows] for b in range(first, first + count)], axis=0)

    def score(index, s_ref):
        q = q_ref[at(index)]
        top = None
        for first in range(0, total, 512):
            cols = slice(first, first + 512)
            part = dot_rows(q, keys(first // rows, 512 // rows))
            if first >= SHORTEST:
                part = part + bias_ref[0:1, cols]
            s_ref[:, cols] = part
            for lane_at in range(0, 512, LANES):
                piece = part[:, lane_at : lane_at + LANES]
                top = piece if top is None else jnp.maximum(top, piece)
        s_ref[:, total:] = top

    def own(index, s_ref):
        @pl.when((index + 1) * QUERIES > length)
        def _():
            for part in range(share):
                block = index * share + part
                start = pl.multiple_of(block * rows, rows)
                raw = dot_rows(q_ref[pl.ds(start, rows)], packed_ref[block, :rows])
                seen = (lane == row) | (lane + start < length)
                raw = jnp.where(seen, raw, FLOOR_SCORE)
                span = slice(part * rows, (part + 1) * rows)
                s_ref[span, pl.ds(start, rows)] = raw
                s_ref[span, total:] = jnp.maximum(s_ref[span, total:], raw)

    def mix(index, s_ref):
        highest = jnp.max(s_ref[:, total:], axis=-1, keepdims=True)
        expo = jnp.exp(s_ref[:, :total] - highest)
        totals = jnp.sum(expo, axis=-1, keepdims=True)
        weights = expo.astype(BF16)
        mixed = jnp.dot(weights, keys(0, blocks), preferred_element_type=F32)
        full_ref[pl.ds(pl.multiple_of(index * QUERIES + AFTER, AFTER), QUERIES)] = half_turn(
            mixed / totals
        ).astype(BF16)

    def near(index, s_ref):
        sums = []
        for part in range(share):
            block = index * share + part
            base = (block * rows).astype(F32)
            begin = jnp.floor((row_f + base + 0.5) / stretch) * stretch
            first = jnp.broadcast_to(jnp.maximum(begin - LEFT, 0.0) - base, (rows, LANES))
            last = jnp.broadcast_to(
                jnp.minimum(begin + stretch + look, float(total)) - base, (rows, LANES)
            )
            span = slice(part * rows, (part + 1) * rows)
            around = (jnp.maximum(block - 1, 0), block, jnp.minimum(block + 1, blocks - 1))
            pieces = []
            for place, other in enumerate(around):
                key_at = lane_f + float((place - 1) * rows)
                if place == 0:
                    inside = key_at >= first
                elif place == 1:
                    inside = (key_at >= first) & (key_at < last)
                else:
                    inside = key_at < last
                raw = s_ref[span, pl.ds(pl.multiple_of(other * rows, rows), rows)]
                pieces.append(jnp.where(inside, raw, FLOOR_SCORE))
            weights, totals = row_softmax(jnp.concatenate(pieces, axis=1))
            w_ref[span, part * rows : (part + 3) * rows] = weights
            sums.append(totals)
        others = [jnp.clip(index * share + b, 0, blocks - 1) for b in range(-1, share + 1)]
        window = jnp.concatenate([packed_ref[b, :rows] for b in others], axis=0)
        mixed = jnp.dot(w_ref[...], window, preferred_element_type=F32)
        near_ref[pl.ds(pl.multiple_of(index * QUERIES + BEFORE, BEFORE), QUERIES)] = (
            mixed / jnp.concatenate(sums, axis=0)
        ).astype(BF16)

    score(0, s0_ref)
    own(0, s0_ref)

    def body(step, carry):
        score(2 * step + 1, s1_ref)
        mix(2 * step, s0_ref)
        near(2 * step, s0_ref)
        own(2 * step + 1, s1_ref)
        score(2 * step + 2, s0_ref)
        mix(2 * step + 1, s1_ref)
        near(2 * step + 1, s1_ref)
        own(2 * step + 2, s0_ref)
        return carry

    lax.fori_loop(0, steps // 2 - 1, body, 0)
    score(steps - 1, s1_ref)
    mix(steps - 2, s0_ref)
    near(jnp.int32(steps - 2), s0_ref)
    own(steps - 1, s1_ref)
    mix(steps - 1, s1_ref)
    near(jnp.int32(steps - 1), s1_ref)
    ext = BEFORE + rows
    low = low_lanes(ext)
    for block in range(blocks):
        span = slice(block * rows, block * rows + ext)
        out_ref[block] = jnp.where(low, full_ref[span], near_ref[span])


def attend(length, stretch, look, packed, before, after):
    blocks, packed_rows, _ = packed.shape
    rows = packed_rows * 2 // 3
    total = blocks * rows
    return pl.pallas_call(
        attend_kernel,
        in_specs=[SMEM_SPEC] * 3 + [VMEM_SPEC] + [pl.BlockSpec(memory_space=pl.ANY)] * 2,
        out_specs=VMEM_SPEC,
        out_shape=jax.ShapeDtypeStruct((blocks, BEFORE + rows, LANES), BF16),
        scratch_shapes=[
            pltpu.VMEM((total, LANES), BF16),
            pltpu.VMEM((8, total), F32),
            pltpu.VMEM((QUERIES, total + LANES), F32),
            pltpu.VMEM((QUERIES, total + LANES), F32),
            pltpu.VMEM((QUERIES, QUERIES + 2 * rows), BF16),
            pltpu.VMEM((total + 2 * AFTER, LANES), BF16),
            pltpu.VMEM((BEFORE + total, LANES), BF16),
        ],
        compiler_params=pltpu.CompilerParams(vmem_limit_bytes=32 << 20),
        name="attend",
    )(length, stretch, look, packed, before, after)


def frame_tile(ref, index):
    return ref[pl.ds(pl.multiple_of(index * TILE, TILE), TILE), :]


def cells(first, tile):
    return pl.ds(first * TILE + tile, TILE, stride=TILE)


def convolve(x_ref, taps, first):
    totals = [None] * STRIDE
    for step in range(STRIDE + KERNEL - 1):
        x = frame_tile(x_ref, first + step)
        for row in range(max(0, step - KERNEL + 1), min(STRIDE, step + 1)):
            term = taps[step - row] * x
            totals[row] = term if totals[row] is None else totals[row] + term
    return totals


def finish_kernel(
    place_ref, length_ref, ctx_ref, before_ref, frames_ref, after_ref, wo_ref, gain_ref, taps_ref,
    full_ref, near_ref, grad_ref,
    c_ref, res_ref, xf_ref, xn_ref, cf_ref, cn_ref, slope_ref, sums_ref,
):
    rows, width = frames_ref.shape
    ext = BEFORE + rows
    length = length_ref[0]
    start = place_ref[0] * rows
    low = low_lanes(ext)
    for pair in range(HEADS // 2):
        cols = slice(pair * LANES, (pair + 1) * LANES)
        one, two = ctx_ref[2 * pair].astype(F32), ctx_ref[2 * pair + 1].astype(F32)
        c_ref[:ext, cols] = jnp.where(low, one, half_turn(two)).astype(BF16)
        c_ref[ext:, cols] = jnp.where(low, half_turn(one), two).astype(BF16)
    frames = frames_ref[...]
    source = jnp.concatenate(
        [before_ref[BEFORE - AFTER :], frames, after_ref[...], before_ref[...], frames], axis=0
    ).astype(F32)
    residual = source + jnp.dot(c_ref[...], wo_ref[...], preferred_element_type=F32)
    res_ref[...] = residual
    normed = norm_rows(residual, gain_ref[...])
    line = lax.broadcasted_iota(jnp.int32, (2 * ext, 1), 0)
    pos = start + jnp.where(line < ext, line - AFTER, line - ext - BEFORE)
    valid = (pos >= 0) & (pos < length)
    x = jnp.where(valid, normed, 0.0).astype(BF16).astype(F32)
    for x_ref, at in ((xf_ref, 0), (xn_ref, ext)):
        for first in range(0, ext, TILE):
            for tile in range(width // LANES):
                x_ref[cells(first, tile), :] = x[
                    at + first : at + first + TILE, tile * LANES : (tile + 1) * LANES
                ]
    full_first = AFTER - KERNEL // 2
    near_first = BEFORE - (KERNEL - 1)

    def conv_rows(step, carry):
        taps = [frame_tile(taps_ref, k) for k in range(KERNEL)]
        at = step * STRIDE
        for x_ref, first, out_ref in ((xf_ref, full_first, cf_ref), (xn_ref, near_first, cn_ref)):
            for row, value in enumerate(convolve(x_ref, taps, at + first)):
                out_ref[pl.ds(pl.multiple_of((at + row) * TILE, TILE), TILE), :] = value
        return carry

    lax.fori_loop(0, rows // STRIDE, conv_rows, 0)
    inner = lax.broadcasted_iota(jnp.int32, (rows, 1), 0) + start
    factor = jnp.where(inner < length, 2.0 / jnp.sqrt(jnp.full((rows, 1), length.astype(F32))), 0.0)
    for tile in range(width // LANES):
        cols = slice(tile * LANES, (tile + 1) * LANES)
        groups = range(0, rows, TILE)
        conv = jnp.concatenate([cf_ref[cells(g, tile), :] for g in groups], axis=0)
        out_full = res_ref[AFTER : AFTER + rows, cols] + conv / (1.0 + jnp.exp(-conv))
        full_ref[:, cols] = out_full.astype(BF16)
        conv = jnp.concatenate([cn_ref[cells(g, tile), :] for g in groups], axis=0)
        sigma = 1.0 / (1.0 + jnp.exp(-conv))
        out_near = res_ref[ext + BEFORE :, cols] + conv * sigma
        near_ref[:, cols] = out_near.astype(BF16)
        slope = (out_near - out_full) * factor * (sigma * (1.0 + conv * (1.0 - sigma)))
        for g in groups:
            slope_ref[cells(g, tile), :] = slope[g : g + TILE]

    def grad_rows(step, sums):
        sums = list(sums)
        at = step * STRIDE
        slopes = [frame_tile(slope_ref, at + row) for row in range(STRIDE)]
        for move in range(STRIDE + KERNEL - 1):
            x = frame_tile(xn_ref, at + near_first + move)
            for row in range(max(0, move - KERNEL + 1), min(STRIDE, move + 1)):
                sums[move - row] = sums[move - row] + slopes[row] * x
        return tuple(sums)

    zero = jnp.zeros((TILE, LANES), F32)
    sums = lax.fori_loop(0, rows // STRIDE, grad_rows, (zero,) * KERNEL)
    for k, value in enumerate(sums + (zero,)):
        sums_ref[k * TILE : (k + 1) * TILE] = value
    for tile in range(width // LANES):
        for part in range(2):
            groups = [sums_ref[cells((2 * part + g) * TILE, tile), :] for g in range(2)]
            grad_ref[2 * tile + part] = jnp.concatenate(groups, axis=0).astype(BF16)


def finish(place, length, ctx, before, frames, after, wo, gain, taps):
    rows, width = frames.shape
    ext = BEFORE + rows
    return pl.pallas_call(
        finish_kernel,
        in_specs=[SMEM_SPEC] * 2 + [VMEM_SPEC] * 7,
        out_specs=[VMEM_SPEC] * 3,
        out_shape=[
            jax.ShapeDtypeStruct((rows, width), BF16),
            jax.ShapeDtypeStruct((rows, width), BF16),
            jax.ShapeDtypeStruct((width // 64, 16, LANES), BF16),
        ],
        scratch_shapes=[
            pltpu.VMEM((2 * ext, width), BF16),
            pltpu.VMEM((2 * ext, width), F32),
            pltpu.VMEM((ext * TILE, LANES), F32),
            pltpu.VMEM((ext * TILE, LANES), F32),
            pltpu.VMEM((rows * TILE, LANES), F32),
            pltpu.VMEM((rows * TILE, LANES), F32),
            pltpu.VMEM((rows * TILE, LANES), F32),
            pltpu.VMEM((32 * TILE, LANES), F32),
        ],
        compiler_params=pltpu.CompilerParams(vmem_limit_bytes=40 << 20),
        name="finish",
    )(place, length, ctx, before, frames, after, wo, gain, taps)


def swap(value, axis):
    return lax.all_to_all(value, axis, 0, 0, tiled=True)


def spread_out(value, axis):
    size = lax.axis_size(axis)
    return swap(jnp.broadcast_to(value[None], (size,) + value.shape), axis)


def add_up(terms):
    total = terms[0].astype(F32)
    for index in range(1, terms.shape[0]):
        total = total + terms[index].astype(F32)
    return total.astype(BF16)


def unfold_kernel(pieces_ref, out_ref):
    taps = out_ref.shape[0]
    for piece in range(pieces_ref.shape[0]):
        tile, part = piece // 2, piece % 2
        value = pieces_ref[piece].astype(F32)
        first = part * value.shape[0]
        count = min(value.shape[0], taps - first)
        out_ref[first : first + count, tile * LANES : (tile + 1) * LANES] = value[:count]


def unfold(pieces):
    return pl.pallas_call(
        unfold_kernel,
        in_specs=[VMEM_SPEC],
        out_specs=VMEM_SPEC,
        out_shape=jax.ShapeDtypeStruct((KERNEL, pieces.shape[0] // 2 * LANES), F32),
        name="unfold",
    )(pieces)


def per_device(
    frames,
    lengths,
    stretch_sizes,
    look_ahead,
    norm_one,
    norm_two,
    w_query,
    w_key,
    w_value,
    w_out,
    conv_kernel,
):
    source = frames[0]
    rows, width = source.shape
    size = lax.axis_size("seq")
    place = lax.axis_index("seq").reshape(1).astype(jnp.int32)
    up = [(i, i + 1) for i in range(size - 1)]
    down = [(j, i) for i, j in up]
    before = lax.ppermute(source[rows - BEFORE :], "seq", up)
    after = lax.ppermute(source[:AFTER], "seq", down)
    taps = conv_kernel.astype(F32).reshape(KERNEL * TILE, LANES)
    packed = project(source, norm_one[None], w_query, w_key, w_value)
    packed = swap(packed, "seq")
    gain = norm_two[None]
    ctx = swap(attend(lengths, stretch_sizes, look_ahead, packed, before, after), "seq")
    full, near, grad = finish(place, lengths, ctx, before, source, after, w_out, gain, taps)
    piece = add_up(swap(grad, "seq"))
    piece = add_up(spread_out(piece, "dp"))
    grads = unfold(spread_out(piece, "seq"))
    return full[None], near[None], grads


def solution(mesh):
    in_specs = (P("dp", "seq", None), P("dp"), P("dp"), P("dp"), P(), P(), P(), P(), P(), P(), P())
    out_specs = (P("dp", "seq", None), P("dp", "seq", None), P())
    return jax.shard_map(
        per_device, mesh=mesh, in_specs=in_specs, out_specs=out_specs, check_vma=False
    )
```

```python
import jax
import jax.numpy as jnp
from jax import lax
from jax.experimental import pallas as pl
from jax.experimental.pallas import tpu as pltpu
from jax.sharding import PartitionSpec as P

HEADS = 16
DEPTH = 64
KERNEL = 31
LEFT = 64
EPSILON = 1e-05
FLOOR_SCORE = -1e30
BEFORE = 32
AFTER = 16
LANES = 128
TILE = 8
STRIDE = 16
PIECES = 4
QUERIES = 512
SHORTEST = 1024
F32 = jnp.float32
BF16 = jnp.bfloat16
SMEM_SPEC = pl.BlockSpec(memory_space=pltpu.SMEM)
VMEM_SPEC = pl.BlockSpec(memory_space=pltpu.VMEM)


def cost(flops, accessed):
    return pl.CostEstimate(flops=flops, bytes_accessed=accessed, transcendentals=0)


def norm_rows(values, gain):
    center = values - jnp.mean(values, axis=-1, keepdims=True)
    spread = jnp.mean(center * center, axis=-1, keepdims=True)
    return center * lax.rsqrt(spread + EPSILON) * gain


def low_lanes(rows):
    return lax.broadcasted_iota(jnp.int32, (rows, LANES), 1) < DEPTH


def half_turn(value):
    return pltpu.roll(value, DEPTH, 1)


def dot_rows(left, right):
    return lax.dot_general(left, right, (((1,), (1,)), ((), ())), preferred_element_type=F32)


def project_kernel(frames_hbm, gain_ref, wq_hbm, wk_hbm, wv_hbm, out_ref, frames_ref, w_ref, sem):
    rows, width = frames_ref.shape
    half = rows // 2
    deep = width // PIECES
    first = pltpu.make_async_copy(frames_hbm, frames_ref, sem.at[3 * PIECES])
    first.start()
    copies = []
    for index, hbm in enumerate((wk_hbm, wv_hbm, wq_hbm)):
        for piece in range(PIECES):
            span = slice(piece * deep, (piece + 1) * deep)
            copy = pltpu.make_async_copy(
                hbm.at[span], w_ref.at[index, span], sem.at[index * PIECES + piece]
            )
            copy.start()
            copies.append(copy)
    first.wait()
    normed = norm_rows(frames_ref[...].astype(F32), gain_ref[...]).astype(BF16)
    products = []
    for index in range(3):
        total = None
        for piece in range(PIECES):
            span = slice(piece * deep, (piece + 1) * deep)
            copies[index * PIECES + piece].wait()
            term = jnp.dot(normed[:, span], w_ref[index, span], preferred_element_type=F32)
            total = term if total is None else total + term
        products.append(total)
    key, value, query = products
    query = query * (DEPTH**-0.5)
    low = low_lanes(rows)
    low_half = low_lanes(half)
    for pair in range(HEADS // 2):
        cols = slice(pair * LANES, (pair + 1) * LANES)
        k, v, q = key[:, cols], value[:, cols], query[:, cols]
        kr, vr, qr = half_turn(k), half_turn(v), half_turn(q)
        out_ref[2 * pair, :rows] = jnp.where(low, k, vr).astype(BF16)
        out_ref[2 * pair + 1, :rows] = jnp.where(low, kr, v).astype(BF16)
        out_ref[2 * pair, rows:] = jnp.where(low_half, q[:half], qr[half:]).astype(BF16)
        out_ref[2 * pair + 1, rows:] = jnp.where(low_half, qr[:half], q[half:]).astype(BF16)


def project(frames, gain, wq, wk, wv):
    rows, width = frames.shape
    hbm = pl.BlockSpec(memory_space=pltpu.HBM)
    return pl.pallas_call(
        project_kernel,
        in_specs=[hbm, VMEM_SPEC, hbm, hbm, hbm],
        out_specs=VMEM_SPEC,
        out_shape=jax.ShapeDtypeStruct((HEADS, rows + rows // 2, LANES), BF16),
        scratch_shapes=[
            pltpu.VMEM((rows, width), BF16),
            pltpu.VMEM((3, width, width), BF16),
            pltpu.SemaphoreType.DMA((3 * PIECES + 1,)),
        ],
        compiler_params=pltpu.CompilerParams(vmem_limit_bytes=62 << 20),
        name="project",
    )(frames, gain, wq, wk, wv)


def row_softmax(scores):
    highest = jnp.max(scores, axis=-1, keepdims=True)
    expo = jnp.exp(scores - highest)
    return expo.astype(BF16), jnp.sum(expo, axis=-1, keepdims=True)


def attend_kernel(
    length_ref, stretch_ref, look_ref, packed_ref, before_ref, after_ref, out_ref,
    q_ref, bias_ref, s0_ref, s1_ref, w_ref, full_ref, near_ref,
):
    blocks, packed_rows, _ = packed_ref.shape
    rows = packed_rows * 2 // 3
    half = rows // 2
    total = blocks * rows
    steps = total // QUERIES
    share = QUERIES // rows
    length = length_ref[0]
    stretch = stretch_ref[0].astype(F32)
    look = look_ref[0].astype(F32)
    low_half = low_lanes(half)
    for block in range(blocks):
        q = packed_ref[block, rows:].astype(F32)
        start = block * rows
        q_ref[start : start + half] = jnp.where(low_half, q, 0.0).astype(BF16)
        q_ref[start + half : start + rows] = jnp.where(low_half, half_turn(q), 0.0).astype(BF16)
    w_ref[...] = jnp.zeros_like(w_ref)
    near_ref[:BEFORE] = jnp.zeros((BEFORE, LANES), BF16)
    full_ref[:AFTER] = jnp.zeros((AFTER, LANES), BF16)
    full_ref[AFTER + total :] = jnp.zeros((AFTER, LANES), BF16)
    key_pos = lax.broadcasted_iota(jnp.int32, (8, total), 1)
    bias_ref[...] = jnp.where(key_pos < length, 0.0, FLOOR_SCORE)
    row = lax.broadcasted_iota(jnp.int32, (rows, LANES), 0)
    lane = lax.broadcasted_iota(jnp.int32, (rows, LANES), 1)
    lane_f = lane.astype(F32)
    row_f = lax.broadcasted_iota(jnp.int32, (rows, 1), 0).astype(F32)

    def at(index):
        return pl.ds(pl.multiple_of(index * QUERIES, QUERIES), QUERIES)

    def keys(first, count):
        return jnp.concatenate([packed_ref[b, :rows] for b in range(first, first + count)], axis=0)

    def score(index, s_ref):
        q = q_ref[at(index)]
        top = None
        for first in range(0, total, 512):
            cols = slice(first, first + 512)
            part = dot_rows(q, keys(first // rows, 512 // rows))
            if first >= SHORTEST:
                part = part + bias_ref[0:1, cols]
            s_ref[:, cols] = part
            for lane_at in range(0, 512, LANES):
                piece = part[:, lane_at : lane_at + LANES]
                top = piece if top is None else jnp.maximum(top, piece)
        s_ref[:, total:] = top

    def own(index, s_ref):
        @pl.when((index + 1) * QUERIES > length)
        def _():
            for part in range(share):
                block = index * share + part
                start = pl.multiple_of(block * rows, rows)
                raw = dot_rows(q_ref[pl.ds(start, rows)], packed_ref[block, :rows])
                seen = (lane == row) | (lane + start < length)
                raw = jnp.where(seen, raw, FLOOR_SCORE)
                span = slice(part * rows, (part + 1) * rows)
                s_ref[span, pl.ds(start, rows)] = raw
                s_ref[span, total:] = jnp.maximum(s_ref[span, total:], raw)

    def mix(index, s_ref):
        highest = jnp.max(s_ref[:, total:], axis=-1, keepdims=True)
        expo = jnp.exp(s_ref[:, :total] - highest)
        totals = jnp.sum(expo, axis=-1, keepdims=True)
        weights = expo.astype(BF16)
        mixed = jnp.dot(weights, keys(0, blocks), preferred_element_type=F32)
        full_ref[pl.ds(pl.multiple_of(index * QUERIES + AFTER, AFTER), QUERIES)] = half_turn(
            mixed / totals
        ).astype(BF16)

    def near(index, s_ref):
        sums = []
        for part in range(share):
            block = index * share + part
            base = (block * rows).astype(F32)
            begin = jnp.floor((row_f + base + 0.5) / stretch) * stretch
            first = jnp.broadcast_to(jnp.maximum(begin - LEFT, 0.0) - base, (rows, LANES))
            last = jnp.broadcast_to(
                jnp.minimum(begin + stretch + look, float(total)) - base, (rows, LANES)
            )
            span = slice(part * rows, (part + 1) * rows)
            around = (jnp.maximum(block - 1, 0), block, jnp.minimum(block + 1, blocks - 1))
            pieces = []
            for place, other in enumerate(around):
                key_at = lane_f + float((place - 1) * rows)
                if place == 0:
                    inside = key_at >= first
                elif place == 1:
                    inside = (key_at >= first) & (key_at < last)
                else:
                    inside = key_at < last
                raw = s_ref[span, pl.ds(pl.multiple_of(other * rows, rows), rows)]
                pieces.append(jnp.where(inside, raw, FLOOR_SCORE))
            weights, totals = row_softmax(jnp.concatenate(pieces, axis=1))
            w_ref[span, part * rows : (part + 3) * rows] = weights
            sums.append(totals)
        others = [jnp.clip(index * share + b, 0, blocks - 1) for b in range(-1, share + 1)]
        window = jnp.concatenate([packed_ref[b, :rows] for b in others], axis=0)
        mixed = jnp.dot(w_ref[...], window, preferred_element_type=F32)
        near_ref[pl.ds(pl.multiple_of(index * QUERIES + BEFORE, BEFORE), QUERIES)] = (
            mixed / jnp.concatenate(sums, axis=0)
        ).astype(BF16)

    score(0, s0_ref)
    own(0, s0_ref)

    def body(step, carry):
        score(2 * step + 1, s1_ref)
        mix(2 * step, s0_ref)
        near(2 * step, s0_ref)
        own(2 * step + 1, s1_ref)
        score(2 * step + 2, s0_ref)
        mix(2 * step + 1, s1_ref)
        near(2 * step + 1, s1_ref)
        own(2 * step + 2, s0_ref)
        return carry

    lax.fori_loop(0, steps // 2 - 1, body, 0)
    score(steps - 1, s1_ref)
    mix(steps - 2, s0_ref)
    near(jnp.int32(steps - 2), s0_ref)
    own(steps - 1, s1_ref)
    mix(steps - 1, s1_ref)
    near(jnp.int32(steps - 1), s1_ref)
    ext = BEFORE + rows
    low = low_lanes(ext)
    for block in range(blocks):
        span = slice(block * rows, block * rows + ext)
        out_ref[block] = jnp.where(low, full_ref[span], near_ref[span])


def attend(length, stretch, look, packed, before, after):
    blocks, packed_rows, _ = packed.shape
    rows = packed_rows * 2 // 3
    total = blocks * rows
    return pl.pallas_call(
        attend_kernel,
        in_specs=[SMEM_SPEC] * 3 + [VMEM_SPEC] + [pl.BlockSpec(memory_space=pl.ANY)] * 2,
        out_specs=VMEM_SPEC,
        out_shape=jax.ShapeDtypeStruct((blocks, BEFORE + rows, LANES), BF16),
        scratch_shapes=[
            pltpu.VMEM((total, LANES), BF16),
            pltpu.VMEM((8, total), F32),
            pltpu.VMEM((QUERIES, total + LANES), F32),
            pltpu.VMEM((QUERIES, total + LANES), F32),
            pltpu.VMEM((QUERIES, QUERIES + 2 * rows), BF16),
            pltpu.VMEM((total + 2 * AFTER, LANES), BF16),
            pltpu.VMEM((BEFORE + total, LANES), BF16),
        ],
        compiler_params=pltpu.CompilerParams(vmem_limit_bytes=32 << 20),
        name="attend",
    )(length, stretch, look, packed, before, after)


def frame_tile(ref, index):
    return ref[pl.ds(pl.multiple_of(index * TILE, TILE), TILE), :]


def cells(first, tile):
    return pl.ds(first * TILE + tile, TILE, stride=TILE)


def convolve(x_ref, taps, first):
    totals = [None] * STRIDE
    for step in range(STRIDE + KERNEL - 1):
        x = frame_tile(x_ref, first + step)
        for row in range(max(0, step - KERNEL + 1), min(STRIDE, step + 1)):
            term = taps[step - row] * x
            totals[row] = term if totals[row] is None else totals[row] + term
    return totals


def finish_kernel(
    place_ref, length_ref, ctx_ref, before_ref, frames_ref, after_ref, wo_ref, gain_ref, taps_ref,
    full_ref, near_ref, grad_ref,
    c_ref, res_ref, xf_ref, xn_ref, cf_ref, cn_ref, slope_ref, sums_ref,
):
    rows, width = frames_ref.shape
    ext = BEFORE + rows
    length = length_ref[0]
    start = place_ref[0] * rows
    low = low_lanes(ext)
    for pair in range(HEADS // 2):
        cols = slice(pair * LANES, (pair + 1) * LANES)
        one, two = ctx_ref[2 * pair].astype(F32), ctx_ref[2 * pair + 1].astype(F32)
        c_ref[:ext, cols] = jnp.where(low, one, half_turn(two)).astype(BF16)
        c_ref[ext:, cols] = jnp.where(low, half_turn(one), two).astype(BF16)
    frames = frames_ref[...]
    source = jnp.concatenate(
        [before_ref[BEFORE - AFTER :], frames, after_ref[...], before_ref[...], frames], axis=0
    ).astype(F32)
    residual = source + jnp.dot(c_ref[...], wo_ref[...], preferred_element_type=F32)
    res_ref[...] = residual
    normed = norm_rows(residual, gain_ref[...])
    line = lax.broadcasted_iota(jnp.int32, (2 * ext, 1), 0)
    pos = start + jnp.where(line < ext, line - AFTER, line - ext - BEFORE)
    valid = (pos >= 0) & (pos < length)
    x = jnp.where(valid, normed, 0.0).astype(BF16).astype(F32)
    for x_ref, at in ((xf_ref, 0), (xn_ref, ext)):
        for first in range(0, ext, TILE):
            for tile in range(width // LANES):
                x_ref[cells(first, tile), :] = x[
                    at + first : at + first + TILE, tile * LANES : (tile + 1) * LANES
                ]
    full_first = AFTER - KERNEL // 2
    near_first = BEFORE - (KERNEL - 1)

    def conv_rows(step, carry):
        taps = [frame_tile(taps_ref, k) for k in range(KERNEL)]
        at = step * STRIDE
        for x_ref, first, out_ref in ((xf_ref, full_first, cf_ref), (xn_ref, near_first, cn_ref)):
            for row, value in enumerate(convolve(x_ref, taps, at + first)):
                out_ref[pl.ds(pl.multiple_of((at + row) * TILE, TILE), TILE), :] = value
        return carry

    lax.fori_loop(0, rows // STRIDE, conv_rows, 0)
    inner = lax.broadcasted_iota(jnp.int32, (rows, 1), 0) + start
    factor = jnp.where(inner < length, 2.0 / jnp.sqrt(jnp.full((rows, 1), length.astype(F32))), 0.0)
    for tile in range(width // LANES):
        cols = slice(tile * LANES, (tile + 1) * LANES)
        groups = range(0, rows, TILE)
        conv = jnp.concatenate([cf_ref[cells(g, tile), :] for g in groups], axis=0)
        out_full = res_ref[AFTER : AFTER + rows, cols] + conv / (1.0 + jnp.exp(-conv))
        full_ref[:, cols] = out_full.astype(BF16)
        conv = jnp.concatenate([cn_ref[cells(g, tile), :] for g in groups], axis=0)
        sigma = 1.0 / (1.0 + jnp.exp(-conv))
        out_near = res_ref[ext + BEFORE :, cols] + conv * sigma
        near_ref[:, cols] = out_near.astype(BF16)
        slope = (out_near - out_full) * factor * (sigma * (1.0 + conv * (1.0 - sigma)))
        for g in groups:
            slope_ref[cells(g, tile), :] = slope[g : g + TILE]

    def grad_rows(step, sums):
        sums = list(sums)
        at = step * STRIDE
        slopes = [frame_tile(slope_ref, at + row) for row in range(STRIDE)]
        for move in range(STRIDE + KERNEL - 1):
            x = frame_tile(xn_ref, at + near_first + move)
            for row in range(max(0, move - KERNEL + 1), min(STRIDE, move + 1)):
                sums[move - row] = sums[move - row] + slopes[row] * x
        return tuple(sums)

    zero = jnp.zeros((TILE, LANES), F32)
    sums = lax.fori_loop(0, rows // STRIDE, grad_rows, (zero,) * KERNEL)
    for k, value in enumerate(sums + (zero,)):
        sums_ref[k * TILE : (k + 1) * TILE] = value
    for tile in range(width // LANES):
        for group in range(4):
            grad_ref[2 * tile + group // 2, group % 2 * TILE : group % 2 * TILE + TILE] = sums_ref[
                cells(group * TILE, tile), :
            ]


def finish(place, length, ctx, before, frames, after, wo, gain, taps):
    rows, width = frames.shape
    ext = BEFORE + rows
    return pl.pallas_call(
        finish_kernel,
        in_specs=[SMEM_SPEC] * 2 + [VMEM_SPEC] * 7,
        out_specs=[VMEM_SPEC] * 3,
        out_shape=[
            jax.ShapeDtypeStruct((rows, width), BF16),
            jax.ShapeDtypeStruct((rows, width), BF16),
            jax.ShapeDtypeStruct((width // 64, 16, LANES), F32),
        ],
        scratch_shapes=[
            pltpu.VMEM((2 * ext, width), BF16),
            pltpu.VMEM((2 * ext, width), F32),
            pltpu.VMEM((ext * TILE, LANES), F32),
            pltpu.VMEM((ext * TILE, LANES), F32),
            pltpu.VMEM((rows * TILE, LANES), F32),
            pltpu.VMEM((rows * TILE, LANES), F32),
            pltpu.VMEM((rows * TILE, LANES), F32),
            pltpu.VMEM((32 * TILE, LANES), F32),
        ],
        compiler_params=pltpu.CompilerParams(vmem_limit_bytes=40 << 20),
        name="finish",
    )(place, length, ctx, before, frames, after, wo, gain, taps)


def swap(value, axis):
    return lax.all_to_all(value, axis, 0, 0, tiled=True)


def spread_out(value, axis):
    size = lax.axis_size(axis)
    return swap(jnp.broadcast_to(value[None], (size,) + value.shape), axis)


def add_up(terms):
    total = terms[0].astype(F32)
    for index in range(1, terms.shape[0]):
        total = total + terms[index].astype(F32)
    return total


def per_device(
    frames,
    lengths,
    stretch_sizes,
    look_ahead,
    norm_one,
    norm_two,
    w_query,
    w_key,
    w_value,
    w_out,
    conv_kernel,
):
    source = frames[0]
    rows, width = source.shape
    size = lax.axis_size("seq")
    place = lax.axis_index("seq").reshape(1).astype(jnp.int32)
    up = [(i, i + 1) for i in range(size - 1)]
    down = [(j, i) for i, j in up]
    before = lax.ppermute(source[rows - BEFORE :], "seq", up)
    after = lax.ppermute(source[:AFTER], "seq", down)
    taps = conv_kernel.astype(F32).reshape(KERNEL * TILE, LANES)
    packed = project(source, norm_one[None], w_query, w_key, w_value)
    packed = swap(packed, "seq")
    gain = norm_two[None]
    ctx = swap(attend(lengths, stretch_sizes, look_ahead, packed, before, after), "seq")
    full, near, grad = finish(place, lengths, ctx, before, source, after, w_out, gain, taps)
    piece = add_up(swap(grad, "seq")).astype(BF16)
    piece = add_up(spread_out(piece, "dp"))
    grads = spread_out(piece, "seq")
    grads = grads.reshape(width // LANES, 32, LANES).transpose(1, 0, 2).reshape(32, width)
    return full[None], near[None], grads[:KERNEL]


def solution(mesh):
    in_specs = (P("dp", "seq", None), P("dp"), P("dp"), P("dp"), P(), P(), P(), P(), P(), P(), P())
    out_specs = (P("dp", "seq", None), P("dp", "seq", None), P())
    return jax.shard_map(
        per_device, mesh=mesh, in_specs=in_specs, out_specs=out_specs, check_vma=False
    )
```

```python
import jax
import jax.numpy as jnp
from jax import lax
from jax.experimental import pallas as pl
from jax.experimental.pallas import tpu as pltpu
from jax.sharding import PartitionSpec as P

HEADS = 16
DEPTH = 64
KERNEL = 31
LEFT = 64
EPSILON = 1e-05
FLOOR_SCORE = -1e30
BEFORE = 32
AFTER = 16
LANES = 128
TILE = 8
STRIDE = 16
PIECES = 4
QUERIES = 512
SHORTEST = 1024
F32 = jnp.float32
BF16 = jnp.bfloat16
SMEM_SPEC = pl.BlockSpec(memory_space=pltpu.SMEM)
VMEM_SPEC = pl.BlockSpec(memory_space=pltpu.VMEM)


def cost(flops, accessed):
    return pl.CostEstimate(flops=flops, bytes_accessed=accessed, transcendentals=0)


def norm_rows(values, gain):
    center = values - jnp.mean(values, axis=-1, keepdims=True)
    spread = jnp.mean(center * center, axis=-1, keepdims=True)
    return center * lax.rsqrt(spread + EPSILON) * gain


def low_lanes(rows):
    return lax.broadcasted_iota(jnp.int32, (rows, LANES), 1) < DEPTH


def half_turn(value):
    return pltpu.roll(value, DEPTH, 1)


def dot_rows(left, right):
    return lax.dot_general(left, right, (((1,), (1,)), ((), ())), preferred_element_type=F32)


def project_kernel(frames_hbm, gain_ref, wq_hbm, wk_hbm, wv_hbm, out_ref, frames_ref, w_ref, sem):
    rows, width = frames_ref.shape
    half = rows // 2
    deep = width // PIECES
    first = pltpu.make_async_copy(frames_hbm, frames_ref, sem.at[3 * PIECES])
    first.start()
    copies = []
    for index, hbm in enumerate((wk_hbm, wv_hbm, wq_hbm)):
        for piece in range(PIECES):
            span = slice(piece * deep, (piece + 1) * deep)
            copy = pltpu.make_async_copy(
                hbm.at[span], w_ref.at[index, span], sem.at[index * PIECES + piece]
            )
            copy.start()
            copies.append(copy)
    first.wait()
    normed = norm_rows(frames_ref[...].astype(F32), gain_ref[...]).astype(BF16)
    products = []
    for index in range(3):
        total = None
        for piece in range(PIECES):
            span = slice(piece * deep, (piece + 1) * deep)
            copies[index * PIECES + piece].wait()
            term = jnp.dot(normed[:, span], w_ref[index, span], preferred_element_type=F32)
            total = term if total is None else total + term
        products.append(total)
    key, value, query = products
    query = query * (DEPTH**-0.5)
    low = low_lanes(rows)
    low_half = low_lanes(half)
    for pair in range(HEADS // 2):
        cols = slice(pair * LANES, (pair + 1) * LANES)
        k, v, q = key[:, cols], value[:, cols], query[:, cols]
        kr, vr, qr = half_turn(k), half_turn(v), half_turn(q)
        out_ref[2 * pair, :rows] = jnp.where(low, k, vr).astype(BF16)
        out_ref[2 * pair + 1, :rows] = jnp.where(low, kr, v).astype(BF16)
        out_ref[2 * pair, rows:] = jnp.where(low_half, q[:half], qr[half:]).astype(BF16)
        out_ref[2 * pair + 1, rows:] = jnp.where(low_half, qr[:half], q[half:]).astype(BF16)


def project(frames, gain, wq, wk, wv):
    rows, width = frames.shape
    hbm = pl.BlockSpec(memory_space=pltpu.HBM)
    return pl.pallas_call(
        project_kernel,
        in_specs=[hbm, VMEM_SPEC, hbm, hbm, hbm],
        out_specs=VMEM_SPEC,
        out_shape=jax.ShapeDtypeStruct((HEADS, rows + rows // 2, LANES), BF16),
        scratch_shapes=[
            pltpu.VMEM((rows, width), BF16),
            pltpu.VMEM((3, width, width), BF16),
            pltpu.SemaphoreType.DMA((3 * PIECES + 1,)),
        ],
        compiler_params=pltpu.CompilerParams(vmem_limit_bytes=62 << 20),
        name="project",
    )(frames, gain, wq, wk, wv)


def row_softmax(scores):
    highest = jnp.max(scores, axis=-1, keepdims=True)
    expo = jnp.exp(scores - highest)
    return expo.astype(BF16), jnp.sum(expo, axis=-1, keepdims=True)


def attend_kernel(
    length_ref, stretch_ref, look_ref, packed_ref, before_ref, after_ref, out_ref,
    q_ref, bias_ref, s0_ref, s1_ref, w_ref, full_ref, near_ref,
):
    blocks, packed_rows, _ = packed_ref.shape
    rows = packed_rows * 2 // 3
    half = rows // 2
    total = blocks * rows
    steps = total // QUERIES
    share = QUERIES // rows
    length = length_ref[0]
    stretch = stretch_ref[0].astype(F32)
    look = look_ref[0].astype(F32)
    low_half = low_lanes(half)
    for block in range(blocks):
        q = packed_ref[block, rows:].astype(F32)
        start = block * rows
        q_ref[start : start + half] = jnp.where(low_half, q, 0.0).astype(BF16)
        q_ref[start + half : start + rows] = jnp.where(low_half, half_turn(q), 0.0).astype(BF16)
    w_ref[...] = jnp.zeros_like(w_ref)
    near_ref[:BEFORE] = jnp.zeros((BEFORE, LANES), BF16)
    full_ref[:AFTER] = jnp.zeros((AFTER, LANES), BF16)
    full_ref[AFTER + total :] = jnp.zeros((AFTER, LANES), BF16)
    key_pos = lax.broadcasted_iota(jnp.int32, (8, total), 1)
    bias_ref[...] = jnp.where(key_pos < length, 0.0, FLOOR_SCORE)
    row = lax.broadcasted_iota(jnp.int32, (rows, LANES), 0)
    lane = lax.broadcasted_iota(jnp.int32, (rows, LANES), 1)
    lane_f = lane.astype(F32)
    row_f = lax.broadcasted_iota(jnp.int32, (rows, 1), 0).astype(F32)

    def at(index):
        return pl.ds(pl.multiple_of(index * QUERIES, QUERIES), QUERIES)

    def keys(first, count):
        return jnp.concatenate([packed_ref[b, :rows] for b in range(first, first + count)], axis=0)

    def score(index, s_ref):
        q = q_ref[at(index)]
        top = None
        for first in range(0, total, 512):
            cols = slice(first, first + 512)
            part = dot_rows(q, keys(first // rows, 512 // rows))
            if first >= SHORTEST:
                part = part + bias_ref[0:1, cols]
            s_ref[:, cols] = part
            for lane_at in range(0, 512, LANES):
                piece = part[:, lane_at : lane_at + LANES]
                top = piece if top is None else jnp.maximum(top, piece)
        s_ref[:, total:] = top

    def own(index, s_ref):
        @pl.when((index + 1) * QUERIES > length)
        def _():
            for part in range(share):
                block = index * share + part
                start = pl.multiple_of(block * rows, rows)
                raw = dot_rows(q_ref[pl.ds(start, rows)], packed_ref[block, :rows])
                seen = (lane == row) | (lane + start < length)
                raw = jnp.where(seen, raw, FLOOR_SCORE)
                span = slice(part * rows, (part + 1) * rows)
                s_ref[span, pl.ds(start, rows)] = raw
                s_ref[span, total:] = jnp.maximum(s_ref[span, total:], raw)

    def mix(index, s_ref):
        highest = jnp.max(s_ref[:, total:], axis=-1, keepdims=True)
        expo = jnp.exp(s_ref[:, :total] - highest)
        totals = jnp.sum(expo, axis=-1, keepdims=True)
        weights = expo.astype(BF16)
        mixed = jnp.dot(weights, keys(0, blocks), preferred_element_type=F32)
        full_ref[pl.ds(pl.multiple_of(index * QUERIES + AFTER, AFTER), QUERIES)] = half_turn(
            mixed / totals
        ).astype(BF16)

    def near(index, s_ref):
        sums = []
        for part in range(share):
            block = index * share + part
            base = (block * rows).astype(F32)
            begin = jnp.floor((row_f + base + 0.5) / stretch) * stretch
            first = jnp.broadcast_to(jnp.maximum(begin - LEFT, 0.0) - base, (rows, LANES))
            last = jnp.broadcast_to(
                jnp.minimum(begin + stretch + look, float(total)) - base, (rows, LANES)
            )
            span = slice(part * rows, (part + 1) * rows)
            around = (jnp.maximum(block - 1, 0), block, jnp.minimum(block + 1, blocks - 1))
            pieces = []
            for place, other in enumerate(around):
                key_at = lane_f + float((place - 1) * rows)
                if place == 0:
                    inside = key_at >= first
                elif place == 1:
                    inside = (key_at >= first) & (key_at < last)
                else:
                    inside = key_at < last
                raw = s_ref[span, pl.ds(pl.multiple_of(other * rows, rows), rows)]
                pieces.append(jnp.where(inside, raw, FLOOR_SCORE))
            weights, totals = row_softmax(jnp.concatenate(pieces, axis=1))
            w_ref[span, part * rows : (part + 3) * rows] = weights
            sums.append(totals)
        others = [jnp.clip(index * share + b, 0, blocks - 1) for b in range(-1, share + 1)]
        window = jnp.concatenate([packed_ref[b, :rows] for b in others], axis=0)
        mixed = jnp.dot(w_ref[...], window, preferred_element_type=F32)
        near_ref[pl.ds(pl.multiple_of(index * QUERIES + BEFORE, BEFORE), QUERIES)] = (
            mixed / jnp.concatenate(sums, axis=0)
        ).astype(BF16)

    score(0, s0_ref)
    own(0, s0_ref)

    def body(step, carry):
        score(2 * step + 1, s1_ref)
        mix(2 * step, s0_ref)
        near(2 * step, s0_ref)
        own(2 * step + 1, s1_ref)
        score(2 * step + 2, s0_ref)
        mix(2 * step + 1, s1_ref)
        near(2 * step + 1, s1_ref)
        own(2 * step + 2, s0_ref)
        return carry

    lax.fori_loop(0, steps // 2 - 1, body, 0)
    score(steps - 1, s1_ref)
    mix(steps - 2, s0_ref)
    near(jnp.int32(steps - 2), s0_ref)
    own(steps - 1, s1_ref)
    mix(steps - 1, s1_ref)
    near(jnp.int32(steps - 1), s1_ref)
    ext = BEFORE + rows
    low = low_lanes(ext)
    for block in range(blocks):
        span = slice(block * rows, block * rows + ext)
        out_ref[block] = jnp.where(low, full_ref[span], near_ref[span])


def attend(length, stretch, look, packed, before, after):
    blocks, packed_rows, _ = packed.shape
    rows = packed_rows * 2 // 3
    total = blocks * rows
    return pl.pallas_call(
        attend_kernel,
        in_specs=[SMEM_SPEC] * 3 + [VMEM_SPEC] + [pl.BlockSpec(memory_space=pl.ANY)] * 2,
        out_specs=VMEM_SPEC,
        out_shape=jax.ShapeDtypeStruct((blocks, BEFORE + rows, LANES), BF16),
        scratch_shapes=[
            pltpu.VMEM((total, LANES), BF16),
            pltpu.VMEM((8, total), F32),
            pltpu.VMEM((QUERIES, total + LANES), F32),
            pltpu.VMEM((QUERIES, total + LANES), F32),
            pltpu.VMEM((QUERIES, QUERIES + 2 * rows), BF16),
            pltpu.VMEM((total + 2 * AFTER, LANES), BF16),
            pltpu.VMEM((BEFORE + total, LANES), BF16),
        ],
        compiler_params=pltpu.CompilerParams(vmem_limit_bytes=32 << 20),
        name="attend",
    )(length, stretch, look, packed, before, after)


def frame_tile(ref, index):
    return ref[pl.ds(pl.multiple_of(index * TILE, TILE), TILE), :]


def cells(first, tile):
    return pl.ds(first * TILE + tile, TILE, stride=TILE)


def convolve(x_ref, taps, first):
    totals = [None] * STRIDE
    for step in range(STRIDE + KERNEL - 1):
        x = frame_tile(x_ref, first + step)
        for row in range(max(0, step - KERNEL + 1), min(STRIDE, step + 1)):
            term = taps[step - row] * x
            totals[row] = term if totals[row] is None else totals[row] + term
    return totals


def finish_kernel(
    place_ref, length_ref, ctx_ref, before_ref, frames_ref, after_ref, wo_ref, gain_ref, taps_ref,
    full_ref, near_ref, grad_ref,
    c_ref, res_ref, xf_ref, xn_ref, cf_ref, cn_ref, slope_ref, sums_ref,
):
    rows, width = frames_ref.shape
    ext = BEFORE + rows
    length = length_ref[0]
    start = place_ref[0] * rows
    low = low_lanes(ext)
    for pair in range(HEADS // 2):
        cols = slice(pair * LANES, (pair + 1) * LANES)
        one, two = ctx_ref[2 * pair].astype(F32), ctx_ref[2 * pair + 1].astype(F32)
        c_ref[:ext, cols] = jnp.where(low, one, half_turn(two)).astype(BF16)
        c_ref[ext:, cols] = jnp.where(low, half_turn(one), two).astype(BF16)
    frames = frames_ref[...]
    source = jnp.concatenate(
        [before_ref[BEFORE - AFTER :], frames, after_ref[...], before_ref[...], frames], axis=0
    ).astype(F32)
    residual = source + jnp.dot(c_ref[...], wo_ref[...], preferred_element_type=F32)
    res_ref[...] = residual
    normed = norm_rows(residual, gain_ref[...])
    line = lax.broadcasted_iota(jnp.int32, (2 * ext, 1), 0)
    pos = start + jnp.where(line < ext, line - AFTER, line - ext - BEFORE)
    valid = (pos >= 0) & (pos < length)
    x = jnp.where(valid, normed, 0.0).astype(BF16).astype(F32)
    for x_ref, at in ((xf_ref, 0), (xn_ref, ext)):
        for first in range(0, ext, TILE):
            for tile in range(width // LANES):
                x_ref[cells(first, tile), :] = x[
                    at + first : at + first + TILE, tile * LANES : (tile + 1) * LANES
                ]
    full_first = AFTER - KERNEL // 2
    near_first = BEFORE - (KERNEL - 1)

    def conv_rows(step, carry):
        taps = [frame_tile(taps_ref, k) for k in range(KERNEL)]
        at = step * STRIDE
        for x_ref, first, out_ref in ((xf_ref, full_first, cf_ref), (xn_ref, near_first, cn_ref)):
            for row, value in enumerate(convolve(x_ref, taps, at + first)):
                out_ref[pl.ds(pl.multiple_of((at + row) * TILE, TILE), TILE), :] = value
        return carry

    lax.fori_loop(0, rows // STRIDE, conv_rows, 0)
    inner = lax.broadcasted_iota(jnp.int32, (rows, 1), 0) + start
    factor = jnp.where(inner < length, 2.0 / jnp.sqrt(jnp.full((rows, 1), length.astype(F32))), 0.0)
    for tile in range(width // LANES):
        cols = slice(tile * LANES, (tile + 1) * LANES)
        groups = range(0, rows, TILE)
        conv = jnp.concatenate([cf_ref[cells(g, tile), :] for g in groups], axis=0)
        out_full = res_ref[AFTER : AFTER + rows, cols] + conv / (1.0 + jnp.exp(-conv))
        full_ref[:, cols] = out_full.astype(BF16)
        conv = jnp.concatenate([cn_ref[cells(g, tile), :] for g in groups], axis=0)
        sigma = 1.0 / (1.0 + jnp.exp(-conv))
        out_near = res_ref[ext + BEFORE :, cols] + conv * sigma
        near_ref[:, cols] = out_near.astype(BF16)
        slope = (out_near - out_full) * factor * (sigma * (1.0 + conv * (1.0 - sigma)))
        for g in groups:
            slope_ref[cells(g, tile), :] = slope[g : g + TILE]

    def grad_rows(step, sums):
        sums = list(sums)
        at = step * STRIDE
        slopes = [frame_tile(slope_ref, at + row) for row in range(STRIDE)]
        for move in range(STRIDE + KERNEL - 1):
            x = frame_tile(xn_ref, at + near_first + move)
            for row in range(max(0, move - KERNEL + 1), min(STRIDE, move + 1)):
                sums[move - row] = sums[move - row] + slopes[row] * x
        return tuple(sums)

    zero = jnp.zeros((TILE, LANES), F32)
    sums = lax.fori_loop(0, rows // STRIDE, grad_rows, (zero,) * KERNEL)
    for k, value in enumerate(sums + (zero,)):
        sums_ref[k * TILE : (k + 1) * TILE] = value
    for group in range(32 // TILE):
        for tile in range(width // LANES):
            grad_ref[group * (width // LANES) + tile] = sums_ref[cells(group * TILE, tile), :]


def finish(place, length, ctx, before, frames, after, wo, gain, taps):
    rows, width = frames.shape
    ext = BEFORE + rows
    return pl.pallas_call(
        finish_kernel,
        in_specs=[SMEM_SPEC] * 2 + [VMEM_SPEC] * 7,
        out_specs=[VMEM_SPEC] * 3,
        out_shape=[
            jax.ShapeDtypeStruct((rows, width), BF16),
            jax.ShapeDtypeStruct((rows, width), BF16),
            jax.ShapeDtypeStruct((32 // TILE * (width // LANES), TILE, LANES), F32),
        ],
        scratch_shapes=[
            pltpu.VMEM((2 * ext, width), BF16),
            pltpu.VMEM((2 * ext, width), F32),
            pltpu.VMEM((ext * TILE, LANES), F32),
            pltpu.VMEM((ext * TILE, LANES), F32),
            pltpu.VMEM((rows * TILE, LANES), F32),
            pltpu.VMEM((rows * TILE, LANES), F32),
            pltpu.VMEM((rows * TILE, LANES), F32),
            pltpu.VMEM((32 * TILE, LANES), F32),
        ],
        compiler_params=pltpu.CompilerParams(vmem_limit_bytes=40 << 20),
        name="finish",
    )(place, length, ctx, before, frames, after, wo, gain, taps)


def swap(value, axis, groups=None):
    return lax.all_to_all(value, axis, 0, 0, tiled=True, axis_index_groups=groups)


def spread_out(value, axis, groups):
    return swap(jnp.broadcast_to(value[None], (len(groups[0]),) + value.shape), axis, groups)


def add_up(terms):
    total = terms[0].astype(F32)
    for index in range(1, terms.shape[0]):
        total = total + terms[index].astype(F32)
    return total


def per_device(
    frames,
    lengths,
    stretch_sizes,
    look_ahead,
    norm_one,
    norm_two,
    w_query,
    w_key,
    w_value,
    w_out,
    conv_kernel,
):
    source = frames[0]
    rows, width = source.shape
    size = lax.axis_size("seq")
    place = lax.axis_index("seq").reshape(1).astype(jnp.int32)
    up = [(i, i + 1) for i in range(size - 1)]
    down = [(j, i) for i, j in up]
    before = lax.ppermute(source[rows - BEFORE :], "seq", up)
    after = lax.ppermute(source[:AFTER], "seq", down)
    taps = conv_kernel.astype(F32).reshape(KERNEL * TILE, LANES)
    packed = project(source, norm_one[None], w_query, w_key, w_value)
    packed = swap(packed, "seq")
    gain = norm_two[None]
    ctx = swap(attend(lengths, stretch_sizes, look_ahead, packed, before, after), "seq")
    full, near, grad = finish(place, lengths, ctx, before, source, after, w_out, gain, taps)
    pairs = lax.axis_size("dp") // 2
    both = ("seq", "dp")
    plane = [[s * 2 * pairs + 2 * z + y for s in range(size) for y in range(2)] for z in range(pairs)]
    column = [[2 * z + y for z in range(pairs)] for y in range(2)]
    piece = add_up(swap(grad, both, plane))
    piece = add_up(spread_out(piece, "dp", column))
    grads = spread_out(piece, both, plane)
    grads = grads.reshape(32 // TILE, width // LANES, TILE, LANES).transpose(0, 2, 1, 3)
    grads = grads.reshape(32, width)
    return full[None], near[None], grads[:KERNEL]


def solution(mesh):
    in_specs = (P("dp", "seq", None), P("dp"), P("dp"), P("dp"), P(), P(), P(), P(), P(), P(), P())
    out_specs = (P("dp", "seq", None), P("dp", "seq", None), P())
    return jax.shard_map(
        per_device, mesh=mesh, in_specs=in_specs, out_specs=out_specs, check_vma=False
    )
```

```python
import jax
import jax.numpy as jnp
from jax import lax
from jax.experimental import pallas as pl
from jax.experimental.pallas import tpu as pltpu
from jax.sharding import PartitionSpec as P

HEADS = 16
DEPTH = 64
KERNEL = 31
LEFT = 64
EPSILON = 1e-05
FLOOR_SCORE = -1e30
BEFORE = 32
AFTER = 16
LANES = 128
TILE = 8
STRIDE = 16
PIECES = 4
QUERIES = 512
SHORTEST = 1024
F32 = jnp.float32
BF16 = jnp.bfloat16
SMEM_SPEC = pl.BlockSpec(memory_space=pltpu.SMEM)
VMEM_SPEC = pl.BlockSpec(memory_space=pltpu.VMEM)


def cost(flops, accessed):
    return pl.CostEstimate(flops=flops, bytes_accessed=accessed, transcendentals=0)


def norm_rows(values, gain):
    center = values - jnp.mean(values, axis=-1, keepdims=True)
    spread = jnp.mean(center * center, axis=-1, keepdims=True)
    return center * lax.rsqrt(spread + EPSILON) * gain


def low_lanes(rows):
    return lax.broadcasted_iota(jnp.int32, (rows, LANES), 1) < DEPTH


def half_turn(value):
    return pltpu.roll(value, DEPTH, 1)


def dot_rows(left, right):
    return lax.dot_general(left, right, (((1,), (1,)), ((), ())), preferred_element_type=F32)


def project_kernel(frames_hbm, gain_ref, wq_hbm, wk_hbm, wv_hbm, out_ref, frames_ref, w_ref, sem):
    rows, width = frames_ref.shape
    half = rows // 2
    deep = width // PIECES
    first = pltpu.make_async_copy(frames_hbm, frames_ref, sem.at[3 * PIECES])
    first.start()
    copies = []
    for index, hbm in enumerate((wk_hbm, wv_hbm, wq_hbm)):
        for piece in range(PIECES):
            span = slice(piece * deep, (piece + 1) * deep)
            copy = pltpu.make_async_copy(
                hbm.at[span], w_ref.at[index, span], sem.at[index * PIECES + piece]
            )
            copy.start()
            copies.append(copy)
    first.wait()
    normed = norm_rows(frames_ref[...].astype(F32), gain_ref[...]).astype(BF16)
    products = []
    for index in range(3):
        total = None
        for piece in range(PIECES):
            span = slice(piece * deep, (piece + 1) * deep)
            copies[index * PIECES + piece].wait()
            term = jnp.dot(normed[:, span], w_ref[index, span], preferred_element_type=F32)
            total = term if total is None else total + term
        products.append(total)
    key, value, query = products
    query = query * (DEPTH**-0.5)
    low = low_lanes(rows)
    low_half = low_lanes(half)
    for pair in range(HEADS // 2):
        cols = slice(pair * LANES, (pair + 1) * LANES)
        k, v, q = key[:, cols], value[:, cols], query[:, cols]
        kr, vr, qr = half_turn(k), half_turn(v), half_turn(q)
        out_ref[2 * pair, :rows] = jnp.where(low, k, vr).astype(BF16)
        out_ref[2 * pair + 1, :rows] = jnp.where(low, kr, v).astype(BF16)
        out_ref[2 * pair, rows:] = jnp.where(low_half, q[:half], qr[half:]).astype(BF16)
        out_ref[2 * pair + 1, rows:] = jnp.where(low_half, qr[:half], q[half:]).astype(BF16)


def project(frames, gain, wq, wk, wv):
    rows, width = frames.shape
    hbm = pl.BlockSpec(memory_space=pltpu.HBM)
    return pl.pallas_call(
        project_kernel,
        in_specs=[hbm, VMEM_SPEC, hbm, hbm, hbm],
        out_specs=VMEM_SPEC,
        out_shape=jax.ShapeDtypeStruct((HEADS, rows + rows // 2, LANES), BF16),
        scratch_shapes=[
            pltpu.VMEM((rows, width), BF16),
            pltpu.VMEM((3, width, width), BF16),
            pltpu.SemaphoreType.DMA((3 * PIECES + 1,)),
        ],
        compiler_params=pltpu.CompilerParams(vmem_limit_bytes=62 << 20),
        name="project",
    )(frames, gain, wq, wk, wv)


def row_softmax(scores):
    highest = jnp.max(scores, axis=-1, keepdims=True)
    expo = jnp.exp(scores - highest)
    return expo.astype(BF16), jnp.sum(expo, axis=-1, keepdims=True)


def attend_kernel(
    length_ref, stretch_ref, look_ref, packed_ref, before_ref, after_ref, out_ref,
    q_ref, bias_ref, s0_ref, s1_ref, w_ref, full_ref, near_ref,
):
    blocks, packed_rows, _ = packed_ref.shape
    rows = packed_rows * 2 // 3
    half = rows // 2
    total = blocks * rows
    steps = total // QUERIES
    share = QUERIES // rows
    length = length_ref[0]
    stretch = stretch_ref[0].astype(F32)
    look = look_ref[0].astype(F32)
    low_half = low_lanes(half)
    for block in range(blocks):
        q = packed_ref[block, rows:].astype(F32)
        start = block * rows
        q_ref[start : start + half] = jnp.where(low_half, q, 0.0).astype(BF16)
        q_ref[start + half : start + rows] = jnp.where(low_half, half_turn(q), 0.0).astype(BF16)
    w_ref[...] = jnp.zeros_like(w_ref)
    near_ref[:BEFORE] = jnp.zeros((BEFORE, LANES), BF16)
    full_ref[:AFTER] = jnp.zeros((AFTER, LANES), BF16)
    full_ref[AFTER + total :] = jnp.zeros((AFTER, LANES), BF16)
    key_pos = lax.broadcasted_iota(jnp.int32, (8, total), 1)
    bias_ref[...] = jnp.where(key_pos < length, 0.0, FLOOR_SCORE)
    row = lax.broadcasted_iota(jnp.int32, (rows, LANES), 0)
    lane = lax.broadcasted_iota(jnp.int32, (rows, LANES), 1)
    lane_f = lane.astype(F32)
    row_f = lax.broadcasted_iota(jnp.int32, (rows, 1), 0).astype(F32)

    def at(index):
        return pl.ds(pl.multiple_of(index * QUERIES, QUERIES), QUERIES)

    def keys(first, count):
        return jnp.concatenate([packed_ref[b, :rows] for b in range(first, first + count)], axis=0)

    def score(index, s_ref):
        q = q_ref[at(index)]
        top = None
        for first in range(0, total, 512):
            cols = slice(first, first + 512)
            part = dot_rows(q, keys(first // rows, 512 // rows))
            if first >= SHORTEST:
                part = part + bias_ref[0:1, cols]
            s_ref[:, cols] = part
            for lane_at in range(0, 512, LANES):
                piece = part[:, lane_at : lane_at + LANES]
                top = piece if top is None else jnp.maximum(top, piece)
        s_ref[:, total:] = top

    def own(index, s_ref):
        @pl.when((index + 1) * QUERIES > length)
        def _():
            for part in range(share):
                block = index * share + part
                start = pl.multiple_of(block * rows, rows)
                raw = dot_rows(q_ref[pl.ds(start, rows)], packed_ref[block, :rows])
                seen = (lane == row) | (lane + start < length)
                raw = jnp.where(seen, raw, FLOOR_SCORE)
                span = slice(part * rows, (part + 1) * rows)
                s_ref[span, pl.ds(start, rows)] = raw
                s_ref[span, total:] = jnp.maximum(s_ref[span, total:], raw)

    def mix(index, s_ref):
        highest = jnp.max(s_ref[:, total:], axis=-1, keepdims=True)
        expo = jnp.exp(s_ref[:, :total] - highest)
        totals = jnp.sum(expo, axis=-1, keepdims=True)
        weights = expo.astype(BF16)
        mixed = jnp.dot(weights, keys(0, blocks), preferred_element_type=F32)
        full_ref[pl.ds(pl.multiple_of(index * QUERIES + AFTER, AFTER), QUERIES)] = half_turn(
            mixed / totals
        ).astype(BF16)

    def near(index, s_ref):
        sums = []
        for part in range(share):
            block = index * share + part
            base = (block * rows).astype(F32)
            begin = jnp.floor((row_f + base + 0.5) / stretch) * stretch
            first = jnp.broadcast_to(jnp.maximum(begin - LEFT, 0.0) - base, (rows, LANES))
            last = jnp.broadcast_to(
                jnp.minimum(begin + stretch + look, float(total)) - base, (rows, LANES)
            )
            span = slice(part * rows, (part + 1) * rows)
            around = (jnp.maximum(block - 1, 0), block, jnp.minimum(block + 1, blocks - 1))
            pieces = []
            for place, other in enumerate(around):
                key_at = lane_f + float((place - 1) * rows)
                if place == 0:
                    inside = key_at >= first
                elif place == 1:
                    inside = (key_at >= first) & (key_at < last)
                else:
                    inside = key_at < last
                raw = s_ref[span, pl.ds(pl.multiple_of(other * rows, rows), rows)]
                pieces.append(jnp.where(inside, raw, FLOOR_SCORE))
            weights, totals = row_softmax(jnp.concatenate(pieces, axis=1))
            own_part = part % 2
            w_ref[span, own_part * rows : (own_part + 3) * rows] = weights
            sums.append(totals)
        mixed = []
        for pair in range(share // 2):
            others = [jnp.clip(index * share + 2 * pair + b, 0, blocks - 1) for b in range(-1, 3)]
            window = jnp.concatenate([packed_ref[b, :rows] for b in others], axis=0)
            span = slice(2 * pair * rows, 2 * (pair + 1) * rows)
            mixed.append(jnp.dot(w_ref[span], window, preferred_element_type=F32))
        mixed = jnp.concatenate(mixed, axis=0)
        near_ref[pl.ds(pl.multiple_of(index * QUERIES + BEFORE, BEFORE), QUERIES)] = (
            mixed / jnp.concatenate(sums, axis=0)
        ).astype(BF16)

    score(0, s0_ref)
    own(0, s0_ref)

    def body(step, carry):
        score(2 * step + 1, s1_ref)
        mix(2 * step, s0_ref)
        near(2 * step, s0_ref)
        own(2 * step + 1, s1_ref)
        score(2 * step + 2, s0_ref)
        mix(2 * step + 1, s1_ref)
        near(2 * step + 1, s1_ref)
        own(2 * step + 2, s0_ref)
        return carry

    lax.fori_loop(0, steps // 2 - 1, body, 0)
    score(steps - 1, s1_ref)
    mix(steps - 2, s0_ref)
    near(jnp.int32(steps - 2), s0_ref)
    own(steps - 1, s1_ref)
    mix(steps - 1, s1_ref)
    near(jnp.int32(steps - 1), s1_ref)
    ext = BEFORE + rows
    low = low_lanes(ext)
    for block in range(blocks):
        span = slice(block * rows, block * rows + ext)
        out_ref[block] = jnp.where(low, full_ref[span], near_ref[span])


def attend(length, stretch, look, packed, before, after):
    blocks, packed_rows, _ = packed.shape
    rows = packed_rows * 2 // 3
    total = blocks * rows
    return pl.pallas_call(
        attend_kernel,
        in_specs=[SMEM_SPEC] * 3 + [VMEM_SPEC] + [pl.BlockSpec(memory_space=pl.ANY)] * 2,
        out_specs=VMEM_SPEC,
        out_shape=jax.ShapeDtypeStruct((blocks, BEFORE + rows, LANES), BF16),
        scratch_shapes=[
            pltpu.VMEM((total, LANES), BF16),
            pltpu.VMEM((8, total), F32),
            pltpu.VMEM((QUERIES, total + LANES), F32),
            pltpu.VMEM((QUERIES, total + LANES), F32),
            pltpu.VMEM((QUERIES, 4 * rows), BF16),
            pltpu.VMEM((total + 2 * AFTER, LANES), BF16),
            pltpu.VMEM((BEFORE + total, LANES), BF16),
        ],
        compiler_params=pltpu.CompilerParams(vmem_limit_bytes=32 << 20),
        name="attend",
    )(length, stretch, look, packed, before, after)


def frame_tile(ref, index):
    return ref[pl.ds(pl.multiple_of(index * TILE, TILE), TILE), :]


def cells(first, tile):
    return pl.ds(first * TILE + tile, TILE, stride=TILE)


def convolve(x_ref, taps, first):
    totals = [None] * STRIDE
    for step in range(STRIDE + KERNEL - 1):
        x = frame_tile(x_ref, first + step)
        for row in range(max(0, step - KERNEL + 1), min(STRIDE, step + 1)):
            term = taps[step - row] * x
            totals[row] = term if totals[row] is None else totals[row] + term
    return totals


def finish_kernel(
    place_ref, length_ref, ctx_ref, before_ref, frames_ref, after_ref, wo_ref, gain_ref, taps_ref,
    full_ref, near_ref, grad_ref,
    c_ref, res_ref, xf_ref, xn_ref, cf_ref, cn_ref, slope_ref, sums_ref,
):
    rows, width = frames_ref.shape
    ext = BEFORE + rows
    length = length_ref[0]
    start = place_ref[0] * rows
    low = low_lanes(ext)
    for pair in range(HEADS // 2):
        cols = slice(pair * LANES, (pair + 1) * LANES)
        one, two = ctx_ref[2 * pair].astype(F32), ctx_ref[2 * pair + 1].astype(F32)
        c_ref[:ext, cols] = jnp.where(low, one, half_turn(two)).astype(BF16)
        c_ref[ext:, cols] = jnp.where(low, half_turn(one), two).astype(BF16)
    frames = frames_ref[...]
    source = jnp.concatenate(
        [before_ref[BEFORE - AFTER :], frames, after_ref[...], before_ref[...], frames], axis=0
    ).astype(F32)
    residual = source + jnp.dot(c_ref[...], wo_ref[...], preferred_element_type=F32)
    res_ref[...] = residual
    normed = norm_rows(residual, gain_ref[...])
    line = lax.broadcasted_iota(jnp.int32, (2 * ext, 1), 0)
    pos = start + jnp.where(line < ext, line - AFTER, line - ext - BEFORE)
    valid = (pos >= 0) & (pos < length)
    x = jnp.where(valid, normed, 0.0).astype(BF16).astype(F32)
    for x_ref, at in ((xf_ref, 0), (xn_ref, ext)):
        for first in range(0, ext, TILE):
            for tile in range(width // LANES):
                x_ref[cells(first, tile), :] = x[
                    at + first : at + first + TILE, tile * LANES : (tile + 1) * LANES
                ]
    full_first = AFTER - KERNEL // 2
    near_first = BEFORE - (KERNEL - 1)

    def conv_rows(step, carry):
        taps = [frame_tile(taps_ref, k) for k in range(KERNEL)]
        at = step * STRIDE
        for x_ref, first, out_ref in ((xf_ref, full_first, cf_ref), (xn_ref, near_first, cn_ref)):
            for row, value in enumerate(convolve(x_ref, taps, at + first)):
                out_ref[pl.ds(pl.multiple_of((at + row) * TILE, TILE), TILE), :] = value
        return carry

    lax.fori_loop(0, rows // STRIDE, conv_rows, 0)
    inner = lax.broadcasted_iota(jnp.int32, (rows, 1), 0) + start
    factor = jnp.where(inner < length, 2.0 / jnp.sqrt(jnp.full((rows, 1), length.astype(F32))), 0.0)
    for tile in range(width // LANES):
        cols = slice(tile * LANES, (tile + 1) * LANES)
        groups = range(0, rows, TILE)
        conv = jnp.concatenate([cf_ref[cells(g, tile), :] for g in groups], axis=0)
        out_full = res_ref[AFTER : AFTER + rows, cols] + conv / (1.0 + jnp.exp(-conv))
        full_ref[:, cols] = out_full.astype(BF16)
        conv = jnp.concatenate([cn_ref[cells(g, tile), :] for g in groups], axis=0)
        sigma = 1.0 / (1.0 + jnp.exp(-conv))
        out_near = res_ref[ext + BEFORE :, cols] + conv * sigma
        near_ref[:, cols] = out_near.astype(BF16)
        slope = (out_near - out_full) * factor * (sigma * (1.0 + conv * (1.0 - sigma)))
        for g in groups:
            slope_ref[cells(g, tile), :] = slope[g : g + TILE]

    def grad_rows(step, sums):
        sums = list(sums)
        at = step * STRIDE
        slopes = [frame_tile(slope_ref, at + row) for row in range(STRIDE)]
        for move in range(STRIDE + KERNEL - 1):
            x = frame_tile(xn_ref, at + near_first + move)
            for row in range(max(0, move - KERNEL + 1), min(STRIDE, move + 1)):
                sums[move - row] = sums[move - row] + slopes[row] * x
        return tuple(sums)

    zero = jnp.zeros((TILE, LANES), F32)
    sums = lax.fori_loop(0, rows // STRIDE, grad_rows, (zero,) * KERNEL)
    for k, value in enumerate(sums + (zero,)):
        sums_ref[k * TILE : (k + 1) * TILE] = value
    for group in range(32 // TILE):
        for tile in range(width // LANES):
            grad_ref[group * (width // LANES) + tile] = sums_ref[cells(group * TILE, tile), :]


def finish(place, length, ctx, before, frames, after, wo, gain, taps):
    rows, width = frames.shape
    ext = BEFORE + rows
    return pl.pallas_call(
        finish_kernel,
        in_specs=[SMEM_SPEC] * 2 + [VMEM_SPEC] * 7,
        out_specs=[VMEM_SPEC] * 3,
        out_shape=[
            jax.ShapeDtypeStruct((rows, width), BF16),
            jax.ShapeDtypeStruct((rows, width), BF16),
            jax.ShapeDtypeStruct((32 // TILE * (width // LANES), TILE, LANES), F32),
        ],
        scratch_shapes=[
            pltpu.VMEM((2 * ext, width), BF16),
            pltpu.VMEM((2 * ext, width), F32),
            pltpu.VMEM((ext * TILE, LANES), F32),
            pltpu.VMEM((ext * TILE, LANES), F32),
            pltpu.VMEM((rows * TILE, LANES), F32),
            pltpu.VMEM((rows * TILE, LANES), F32),
            pltpu.VMEM((rows * TILE, LANES), F32),
            pltpu.VMEM((32 * TILE, LANES), F32),
        ],
        compiler_params=pltpu.CompilerParams(vmem_limit_bytes=40 << 20),
        name="finish",
    )(place, length, ctx, before, frames, after, wo, gain, taps)


def swap(value, axis, groups=None):
    return lax.all_to_all(value, axis, 0, 0, tiled=True, axis_index_groups=groups)


def spread_out(value, axis, groups):
    return swap(jnp.broadcast_to(value[None], (len(groups[0]),) + value.shape), axis, groups)


def add_up(terms):
    total = terms[0].astype(F32)
    for index in range(1, terms.shape[0]):
        total = total + terms[index].astype(F32)
    return total


def per_device(
    frames,
    lengths,
    stretch_sizes,
    look_ahead,
    norm_one,
    norm_two,
    w_query,
    w_key,
    w_value,
    w_out,
    conv_kernel,
):
    source = frames[0]
    rows, width = source.shape
    size = lax.axis_size("seq")
    place = lax.axis_index("seq").reshape(1).astype(jnp.int32)
    up = [(i, i + 1) for i in range(size - 1)]
    down = [(j, i) for i, j in up]
    before = lax.ppermute(source[rows - BEFORE :], "seq", up)
    after = lax.ppermute(source[:AFTER], "seq", down)
    taps = conv_kernel.astype(F32).reshape(KERNEL * TILE, LANES)
    packed = project(source, norm_one[None], w_query, w_key, w_value)
    packed = swap(packed, "seq")
    gain = norm_two[None]
    ctx = swap(attend(lengths, stretch_sizes, look_ahead, packed, before, after), "seq")
    full, near, grad = finish(place, lengths, ctx, before, source, after, w_out, gain, taps)
    pairs = lax.axis_size("dp") // 2
    both = ("seq", "dp")
    plane = [[s * 2 * pairs + 2 * z + y for s in range(size) for y in range(2)] for z in range(pairs)]
    column = [[2 * z + y for z in range(pairs)] for y in range(2)]
    piece = add_up(swap(grad, both, plane))
    piece = add_up(spread_out(piece, "dp", column))
    grads = spread_out(piece, both, plane)
    grads = grads.reshape(32 // TILE, width // LANES, TILE, LANES).transpose(0, 2, 1, 3)
    grads = grads.reshape(32, width)
    return full[None], near[None], grads[:KERNEL]


def solution(mesh):
    in_specs = (P("dp", "seq", None), P("dp"), P("dp"), P("dp"), P(), P(), P(), P(), P(), P(), P())
    out_specs = (P("dp", "seq", None), P("dp", "seq", None), P())
    return jax.shard_map(
        per_device, mesh=mesh, in_specs=in_specs, out_specs=out_specs, check_vma=False
    )
```

```python
import jax
import jax.numpy as jnp
from jax import lax
from jax.experimental import pallas as pl
from jax.experimental.pallas import tpu as pltpu
from jax.sharding import PartitionSpec as P

HEADS = 16
DEPTH = 64
KERNEL = 31
LEFT = 64
EPSILON = 1e-05
FLOOR_SCORE = -1e30
BEFORE = 32
AFTER = 16
LANES = 128
TILE = 8
STRIDE = 16
PIECES = 4
QUERIES = 512
SHORTEST = 1024
F32 = jnp.float32
BF16 = jnp.bfloat16
SMEM_SPEC = pl.BlockSpec(memory_space=pltpu.SMEM)
VMEM_SPEC = pl.BlockSpec(memory_space=pltpu.VMEM)


def cost(flops, accessed):
    return pl.CostEstimate(flops=flops, bytes_accessed=accessed, transcendentals=0)


def norm_rows(values, gain):
    center = values - jnp.mean(values, axis=-1, keepdims=True)
    spread = jnp.mean(center * center, axis=-1, keepdims=True)
    return center * lax.rsqrt(spread + EPSILON) * gain


def low_lanes(rows):
    return lax.broadcasted_iota(jnp.int32, (rows, LANES), 1) < DEPTH


def half_turn(value):
    return pltpu.roll(value, DEPTH, 1)


def dot_rows(left, right):
    return lax.dot_general(left, right, (((1,), (1,)), ((), ())), preferred_element_type=F32)


def project_kernel(frames_hbm, gain_ref, wq_hbm, wk_hbm, wv_hbm, out_ref, frames_ref, w_ref, sem):
    rows, width = frames_ref.shape
    half = rows // 2
    deep = width // PIECES
    first = pltpu.make_async_copy(frames_hbm, frames_ref, sem.at[3 * PIECES])
    first.start()
    copies = []
    for index, hbm in enumerate((wk_hbm, wv_hbm, wq_hbm)):
        for piece in range(PIECES):
            span = slice(piece * deep, (piece + 1) * deep)
            copy = pltpu.make_async_copy(
                hbm.at[span], w_ref.at[index, span], sem.at[index * PIECES + piece]
            )
            copy.start()
            copies.append(copy)
    first.wait()
    normed = norm_rows(frames_ref[...].astype(F32), gain_ref[...]).astype(BF16)
    products = []
    for index in range(3):
        total = None
        for piece in range(PIECES):
            span = slice(piece * deep, (piece + 1) * deep)
            copies[index * PIECES + piece].wait()
            term = jnp.dot(normed[:, span], w_ref[index, span], preferred_element_type=F32)
            total = term if total is None else total + term
        products.append(total)
    key, value, query = products
    query = query * (DEPTH**-0.5)
    low = low_lanes(rows)
    low_half = low_lanes(half)
    for pair in range(HEADS // 2):
        cols = slice(pair * LANES, (pair + 1) * LANES)
        k, v, q = key[:, cols], value[:, cols], query[:, cols]
        kr, vr, qr = half_turn(k), half_turn(v), half_turn(q)
        out_ref[2 * pair, :rows] = jnp.where(low, k, vr).astype(BF16)
        out_ref[2 * pair + 1, :rows] = jnp.where(low, kr, v).astype(BF16)
        out_ref[2 * pair, rows:] = jnp.where(low_half, q[:half], qr[half:]).astype(BF16)
        out_ref[2 * pair + 1, rows:] = jnp.where(low_half, qr[:half], q[half:]).astype(BF16)


def project(frames, gain, wq, wk, wv):
    rows, width = frames.shape
    hbm = pl.BlockSpec(memory_space=pltpu.HBM)
    return pl.pallas_call(
        project_kernel,
        in_specs=[hbm, VMEM_SPEC, hbm, hbm, hbm],
        out_specs=VMEM_SPEC,
        out_shape=jax.ShapeDtypeStruct((HEADS, rows + rows // 2, LANES), BF16),
        scratch_shapes=[
            pltpu.VMEM((rows, width), BF16),
            pltpu.VMEM((3, width, width), BF16),
            pltpu.SemaphoreType.DMA((3 * PIECES + 1,)),
        ],
        compiler_params=pltpu.CompilerParams(vmem_limit_bytes=62 << 20),
        name="project",
    )(frames, gain, wq, wk, wv)


def row_softmax(scores):
    highest = jnp.max(scores, axis=-1, keepdims=True)
    expo = jnp.exp(scores - highest)
    return expo.astype(BF16), jnp.sum(expo, axis=-1, keepdims=True)


def attend_kernel(
    length_ref, stretch_ref, look_ref, packed_ref, before_ref, out_ref,
    q_ref, bias_ref, s0_ref, s1_ref, w_ref, full_ref, near_ref,
):
    blocks, packed_rows, _ = packed_ref.shape
    rows = packed_rows * 2 // 3
    half = rows // 2
    total = blocks * rows
    steps = total // QUERIES
    share = QUERIES // rows
    length = length_ref[0]
    stretch = stretch_ref[0].astype(F32)
    look = look_ref[0].astype(F32)
    low_half = low_lanes(half)
    for block in range(blocks):
        q = packed_ref[block, rows:].astype(F32)
        start = block * rows
        q_ref[start : start + half] = jnp.where(low_half, q, 0.0).astype(BF16)
        q_ref[start + half : start + rows] = jnp.where(low_half, half_turn(q), 0.0).astype(BF16)
    w_ref[...] = jnp.zeros_like(w_ref)
    near_ref[:BEFORE] = jnp.zeros((BEFORE, LANES), BF16)
    full_ref[:AFTER] = jnp.zeros((AFTER, LANES), BF16)
    full_ref[AFTER + total :] = jnp.zeros((AFTER, LANES), BF16)
    key_pos = lax.broadcasted_iota(jnp.int32, (8, total), 1)
    bias_ref[...] = jnp.where(key_pos < length, 0.0, FLOOR_SCORE)
    row = lax.broadcasted_iota(jnp.int32, (rows, LANES), 0)
    lane = lax.broadcasted_iota(jnp.int32, (rows, LANES), 1)
    lane_f = lane.astype(F32)
    row_f = lax.broadcasted_iota(jnp.int32, (rows, 1), 0).astype(F32)

    def at(index):
        return pl.ds(pl.multiple_of(index * QUERIES, QUERIES), QUERIES)

    def keys(first, count):
        return jnp.concatenate([packed_ref[b, :rows] for b in range(first, first + count)], axis=0)

    def score(index, s_ref):
        q = q_ref[at(index)]
        top = None
        for first in range(0, total, 512):
            cols = slice(first, first + 512)
            part = dot_rows(q, keys(first // rows, 512 // rows))
            if first >= SHORTEST:
                part = part + bias_ref[0:1, cols]
            s_ref[:, cols] = part
            for lane_at in range(0, 512, LANES):
                piece = part[:, lane_at : lane_at + LANES]
                top = piece if top is None else jnp.maximum(top, piece)
        s_ref[:, total:] = top

    def own(index, s_ref):
        @pl.when((index + 1) * QUERIES > length)
        def _():
            for part in range(share):
                block = index * share + part
                start = pl.multiple_of(block * rows, rows)
                raw = dot_rows(q_ref[pl.ds(start, rows)], packed_ref[block, :rows])
                seen = (lane == row) | (lane + start < length)
                raw = jnp.where(seen, raw, FLOOR_SCORE)
                span = slice(part * rows, (part + 1) * rows)
                s_ref[span, pl.ds(start, rows)] = raw
                s_ref[span, total:] = jnp.maximum(s_ref[span, total:], raw)

    def mix(index, s_ref):
        highest = jnp.max(s_ref[:, total:], axis=-1, keepdims=True)
        expo = jnp.exp(s_ref[:, :total] - highest)
        totals = jnp.sum(expo, axis=-1, keepdims=True)
        weights = expo.astype(BF16)
        mixed = jnp.dot(weights, keys(0, blocks), preferred_element_type=F32)
        full_ref[pl.ds(pl.multiple_of(index * QUERIES + AFTER, AFTER), QUERIES)] = half_turn(
            mixed / totals
        ).astype(BF16)

    def near(index, s_ref):
        sums = []
        for part in range(share):
            block = index * share + part
            base = (block * rows).astype(F32)
            begin = jnp.floor((row_f + base + 0.5) / stretch) * stretch
            first = jnp.broadcast_to(jnp.maximum(begin - LEFT, 0.0) - base, (rows, LANES))
            last = jnp.broadcast_to(
                jnp.minimum(begin + stretch + look, float(total)) - base, (rows, LANES)
            )
            span = slice(part * rows, (part + 1) * rows)
            around = (jnp.maximum(block - 1, 0), block, jnp.minimum(block + 1, blocks - 1))
            pieces = []
            for place, other in enumerate(around):
                key_at = lane_f + float((place - 1) * rows)
                if place == 0:
                    inside = key_at >= first
                elif place == 1:
                    inside = (key_at >= first) & (key_at < last)
                else:
                    inside = key_at < last
                raw = s_ref[span, pl.ds(pl.multiple_of(other * rows, rows), rows)]
                pieces.append(jnp.where(inside, raw, FLOOR_SCORE))
            weights, totals = row_softmax(jnp.concatenate(pieces, axis=1))
            own_part = part % 2
            w_ref[span, own_part * rows : (own_part + 3) * rows] = weights
            sums.append(totals)
        mixed = []
        for pair in range(share // 2):
            others = [jnp.clip(index * share + 2 * pair + b, 0, blocks - 1) for b in range(-1, 3)]
            window = jnp.concatenate([packed_ref[b, :rows] for b in others], axis=0)
            span = slice(2 * pair * rows, 2 * (pair + 1) * rows)
            mixed.append(jnp.dot(w_ref[span], window, preferred_element_type=F32))
        mixed = jnp.concatenate(mixed, axis=0)
        near_ref[pl.ds(pl.multiple_of(index * QUERIES + BEFORE, BEFORE), QUERIES)] = (
            mixed / jnp.concatenate(sums, axis=0)
        ).astype(BF16)

    score(0, s0_ref)
    own(0, s0_ref)

    def body(step, carry):
        score(2 * step + 1, s1_ref)
        mix(2 * step, s0_ref)
        near(2 * step, s0_ref)
        own(2 * step + 1, s1_ref)
        score(2 * step + 2, s0_ref)
        mix(2 * step + 1, s1_ref)
        near(2 * step + 1, s1_ref)
        own(2 * step + 2, s0_ref)
        return carry

    lax.fori_loop(0, steps // 2 - 1, body, 0)
    score(steps - 1, s1_ref)
    mix(steps - 2, s0_ref)
    near(jnp.int32(steps - 2), s0_ref)
    own(steps - 1, s1_ref)
    mix(steps - 1, s1_ref)
    near(jnp.int32(steps - 1), s1_ref)
    ext = BEFORE + rows
    low = low_lanes(ext)
    for block in range(blocks):
        span = slice(block * rows, block * rows + ext)
        out_ref[block] = jnp.where(low, full_ref[span], near_ref[span])


def attend(length, stretch, look, packed, before):
    blocks, packed_rows, _ = packed.shape
    rows = packed_rows * 2 // 3
    total = blocks * rows
    return pl.pallas_call(
        attend_kernel,
        in_specs=[SMEM_SPEC] * 3 + [VMEM_SPEC] + [pl.BlockSpec(memory_space=pl.ANY)],
        out_specs=VMEM_SPEC,
        out_shape=jax.ShapeDtypeStruct((blocks, BEFORE + rows, LANES), BF16),
        scratch_shapes=[
            pltpu.VMEM((total, LANES), BF16),
            pltpu.VMEM((8, total), F32),
            pltpu.VMEM((QUERIES, total + LANES), F32),
            pltpu.VMEM((QUERIES, total + LANES), F32),
            pltpu.VMEM((QUERIES, 4 * rows), BF16),
            pltpu.VMEM((total + 2 * AFTER, LANES), BF16),
            pltpu.VMEM((BEFORE + total, LANES), BF16),
        ],
        compiler_params=pltpu.CompilerParams(vmem_limit_bytes=32 << 20),
        name="attend",
    )(length, stretch, look, packed, before)


def frame_tile(ref, index):
    return ref[pl.ds(pl.multiple_of(index * TILE, TILE), TILE), :]


def cells(first, tile):
    return pl.ds(first * TILE + tile, TILE, stride=TILE)


def convolve(x_ref, taps, first):
    totals = [None] * STRIDE
    for step in range(STRIDE + KERNEL - 1):
        x = frame_tile(x_ref, first + step)
        for row in range(max(0, step - KERNEL + 1), min(STRIDE, step + 1)):
            term = taps[step - row] * x
            totals[row] = term if totals[row] is None else totals[row] + term
    return totals


def finish_kernel(
    place_ref, length_ref, ctx_ref, before_ref, frames_ref, after_ref, wo_ref, gain_ref, taps_ref,
    full_ref, near_ref, grad_ref,
    c_ref, res_ref, xf_ref, xn_ref, cf_ref, cn_ref, slope_ref, sums_ref,
):
    rows, width = frames_ref.shape
    ext = BEFORE + rows
    length = length_ref[0]
    start = place_ref[0] * rows
    low = low_lanes(ext)
    for pair in range(HEADS // 2):
        cols = slice(pair * LANES, (pair + 1) * LANES)
        one, two = ctx_ref[2 * pair].astype(F32), ctx_ref[2 * pair + 1].astype(F32)
        c_ref[:ext, cols] = jnp.where(low, one, half_turn(two)).astype(BF16)
        c_ref[ext:, cols] = jnp.where(low, half_turn(one), two).astype(BF16)
    frames = frames_ref[...]
    source = jnp.concatenate(
        [before_ref[BEFORE - AFTER :], frames, after_ref[...], before_ref[...], frames], axis=0
    ).astype(F32)
    residual = source + jnp.dot(c_ref[...], wo_ref[...], preferred_element_type=F32)
    res_ref[...] = residual
    normed = norm_rows(residual, gain_ref[...])
    line = lax.broadcasted_iota(jnp.int32, (2 * ext, 1), 0)
    pos = start + jnp.where(line < ext, line - AFTER, line - ext - BEFORE)
    valid = (pos >= 0) & (pos < length)
    x = jnp.where(valid, normed, 0.0).astype(BF16).astype(F32)
    for x_ref, at in ((xf_ref, 0), (xn_ref, ext)):
        for first in range(0, ext, TILE):
            for tile in range(width // LANES):
                x_ref[cells(first, tile), :] = x[
                    at + first : at + first + TILE, tile * LANES : (tile + 1) * LANES
                ]
    full_first = AFTER - KERNEL // 2
    near_first = BEFORE - (KERNEL - 1)

    def conv_rows(step, carry):
        taps = [frame_tile(taps_ref, k) for k in range(KERNEL)]
        at = step * STRIDE
        for x_ref, first, out_ref in ((xf_ref, full_first, cf_ref), (xn_ref, near_first, cn_ref)):
            for row, value in enumerate(convolve(x_ref, taps, at + first)):
                out_ref[pl.ds(pl.multiple_of((at + row) * TILE, TILE), TILE), :] = value
        return carry

    lax.fori_loop(0, rows // STRIDE, conv_rows, 0)
    inner = lax.broadcasted_iota(jnp.int32, (rows, 1), 0) + start
    factor = jnp.where(inner < length, 2.0 / jnp.sqrt(jnp.full((rows, 1), length.astype(F32))), 0.0)
    for tile in range(width // LANES):
        cols = slice(tile * LANES, (tile + 1) * LANES)
        groups = range(0, rows, TILE)
        conv = jnp.concatenate([cf_ref[cells(g, tile), :] for g in groups], axis=0)
        out_full = res_ref[AFTER : AFTER + rows, cols] + conv / (1.0 + jnp.exp(-conv))
        full_ref[:, cols] = out_full.astype(BF16)
        conv = jnp.concatenate([cn_ref[cells(g, tile), :] for g in groups], axis=0)
        sigma = 1.0 / (1.0 + jnp.exp(-conv))
        out_near = res_ref[ext + BEFORE :, cols] + conv * sigma
        near_ref[:, cols] = out_near.astype(BF16)
        slope = (out_near - out_full) * factor * (sigma * (1.0 + conv * (1.0 - sigma)))
        for g in groups:
            slope_ref[cells(g, tile), :] = slope[g : g + TILE]

    def grad_rows(step, sums):
        sums = list(sums)
        at = step * STRIDE
        slopes = [frame_tile(slope_ref, at + row) for row in range(STRIDE)]
        for move in range(STRIDE + KERNEL - 1):
            x = frame_tile(xn_ref, at + near_first + move)
            for row in range(max(0, move - KERNEL + 1), min(STRIDE, move + 1)):
                sums[move - row] = sums[move - row] + slopes[row] * x
        return tuple(sums)

    zero = jnp.zeros((TILE, LANES), F32)
    sums = lax.fori_loop(0, rows // STRIDE, grad_rows, (zero,) * KERNEL)
    for k, value in enumerate(sums + (zero,)):
        sums_ref[k * TILE : (k + 1) * TILE] = value
    for group in range(32 // TILE):
        for tile in range(width // LANES):
            grad_ref[group * (width // LANES) + tile] = sums_ref[cells(group * TILE, tile), :]


def finish(place, length, ctx, before, frames, after, wo, gain, taps):
    rows, width = frames.shape
    ext = BEFORE + rows
    return pl.pallas_call(
        finish_kernel,
        in_specs=[SMEM_SPEC] * 2 + [VMEM_SPEC] * 7,
        out_specs=[VMEM_SPEC] * 3,
        out_shape=[
            jax.ShapeDtypeStruct((rows, width), BF16),
            jax.ShapeDtypeStruct((rows, width), BF16),
            jax.ShapeDtypeStruct((32 // TILE * (width // LANES), TILE, LANES), F32),
        ],
        scratch_shapes=[
            pltpu.VMEM((2 * ext, width), BF16),
            pltpu.VMEM((2 * ext, width), F32),
            pltpu.VMEM((ext * TILE, LANES), F32),
            pltpu.VMEM((ext * TILE, LANES), F32),
            pltpu.VMEM((rows * TILE, LANES), F32),
            pltpu.VMEM((rows * TILE, LANES), F32),
            pltpu.VMEM((rows * TILE, LANES), F32),
            pltpu.VMEM((32 * TILE, LANES), F32),
        ],
        compiler_params=pltpu.CompilerParams(vmem_limit_bytes=40 << 20),
        name="finish",
    )(place, length, ctx, before, frames, after, wo, gain, taps)


def swap(value, axis, groups=None):
    return lax.all_to_all(value, axis, 0, 0, tiled=True, axis_index_groups=groups)


def spread_out(value, axis, groups):
    return swap(jnp.broadcast_to(value[None], (len(groups[0]),) + value.shape), axis, groups)


def add_up(terms):
    total = terms[0].astype(F32)
    for index in range(1, terms.shape[0]):
        total = total + terms[index].astype(F32)
    return total


def per_device(
    frames,
    lengths,
    stretch_sizes,
    look_ahead,
    norm_one,
    norm_two,
    w_query,
    w_key,
    w_value,
    w_out,
    conv_kernel,
):
    source = frames[0]
    rows, width = source.shape
    size = lax.axis_size("seq")
    place = lax.axis_index("seq").reshape(1).astype(jnp.int32)
    up = [(i, i + 1) for i in range(size - 1)]
    down = [(j, i) for i, j in up]
    before = lax.ppermute(source[rows - BEFORE :], "seq", up)
    after = lax.ppermute(source[:AFTER], "seq", down)
    taps = conv_kernel.astype(F32).reshape(KERNEL * TILE, LANES)
    packed = project(source, norm_one[None], w_query, w_key, w_value)
    packed = swap(packed, "seq")
    gain = norm_two[None]
    ctx = swap(attend(lengths, stretch_sizes, look_ahead, packed, before), "seq")
    full, near, grad = finish(place, lengths, ctx, before, source, after, w_out, gain, taps)
    pairs = lax.axis_size("dp") // 2
    both = ("seq", "dp")
    plane = [[s * 2 * pairs + 2 * z + y for s in range(size) for y in range(2)] for z in range(pairs)]
    column = [[2 * z + y for z in range(pairs)] for y in range(2)]
    piece = add_up(swap(grad, both, plane))
    piece = add_up(spread_out(piece, "dp", column))
    grads = spread_out(piece, both, plane)
    grads = grads.reshape(32 // TILE, width // LANES, TILE, LANES).transpose(0, 2, 1, 3)
    grads = grads.reshape(32, width)
    return full[None], near[None], grads[:KERNEL]


def solution(mesh):
    in_specs = (P("dp", "seq", None), P("dp"), P("dp"), P("dp"), P(), P(), P(), P(), P(), P(), P())
    out_specs = (P("dp", "seq", None), P("dp", "seq", None), P())
    return jax.shard_map(
        per_device, mesh=mesh, in_specs=in_specs, out_specs=out_specs, check_vma=False
    )
```
